256 devices in a mesh: section: 8 (over x, y_lo), tp: 32 (over z, y_hi, core).
Axes of the slice: x: 4, y: 4 (y_hi: 2, y_lo: 2; y = y_hi * 2 + y_lo), z: 8, core: 2. Of those that a mesh axis runs over, the one named last changes fastest.
Arguments:
- resid: bfloat16 [8, 512, 8192], P('section', 'tp'), may hold values from -36 to 36
- pending: bfloat16 [8, 512, 8192], P('section', 'tp'), may hold values from -6 to 6
- doc_ids: int32 [8, 512], P('section'), may hold values from 0 to 3, never falling along the last dimension, each value on 1 to 256 neighbouring positions
- norm_gain: bfloat16 [8, 8192], P('section'), may hold values from 0.25 to 1.75
- q_weight: bfloat16 [8, 8192, 8192], P('section', None, 'tp'), may hold values from -2 to 2
- kv_weight: bfloat16 [8, 8192, 1024], P('section', None, 'tp'), may hold values from -1 to 1
- o_weight: bfloat16 [8, 8192, 8192], P('section', 'tp'), may hold values from -0.25 to 0.25
Outputs:
- next_resid: bfloat16 [8, 512, 8192], P('section', 'tp')
- next_output: bfloat16 [8, 512, 8192], P('section', 'tp')
The draws below stay inside these ranges and needn't reach their ends.
Inputs may be any that keep to these rules, and one draw needn't show every extreme that they name: `doc_ids`: ids never fall along the tokens of a micro-batch; every document has 1 to 256 tokens, and one has exactly that many.
All inputs are finite; a program needn't handle non-finite values.
Results may differ from the reference program's by a relative error of at most 0.03.
Values may be sent and summed in bfloat16 or wider, within the bound.
A program may use at most 128 MiB of HBM per device.

```python
import math
import jax
import jax.numpy as jnp
import numpy as np
from jax import lax

D = 8192
HEADS = 64
KV_HEADS = 4
HD = 128
DOCS = 4
TOKENS = 512
SECTIONS = 8
N_TP = 32


def keyval_base(key):
    base = jax.random.normal(key, (SECTIONS, D, 2 * KV_HEADS * HD), jnp.float32)
    return jnp.clip(base, -6.0, 6.0) * D ** (-0.5)


def draw_kv_weight(key, part):
    base = keyval_base(key)
    return jnp.clip(base, -1.0, 1.0).astype(jnp.bfloat16)


def draw_q_weight(key, part):
    key = jax.random.fold_in(key, 3)
    noise = jnp.clip(jax.random.normal(key, (SECTIONS, D, HEADS * HD), jnp.float32), -6.0, 6.0) * D ** (-0.5)
    return jnp.clip(noise, -2.0, 2.0).astype(jnp.bfloat16)


def draw_resid(key, part):
    key = jax.random.fold_in(key, 5)
    key_base, key_rows, key_cols = jax.random.split(key, 3)
    shape = (SECTIONS, TOKENS, D)
    base = jnp.clip(jax.random.normal(key_base, shape, jnp.float32), -4.0, 4.0)
    row_scale = jnp.exp(jax.random.uniform(key_rows, (SECTIONS, TOKENS, 1), jnp.float32, math.log(0.3), math.log(3.0)))
    col_scale = jnp.exp(jax.random.uniform(key_cols, (SECTIONS, 1, D), jnp.float32, math.log(0.3), math.log(3.0)))
    values = base * row_scale * col_scale
    return jnp.clip(values, -36.0, 36.0).astype(jnp.bfloat16)


def shard_levels(stream_key, extent, shards, smallest, largest):
    def one(position, parts):
        heights = jax.random.uniform(jax.random.fold_in(jax.random.fold_in(stream_key, 6), position), (parts,), jnp.float32, smallest / len(shards), largest / len(shards))
        return jnp.repeat(jnp.exp(heights), extent[position] // parts).reshape((-1,) + (1,) * (len(extent) - position - 1))

    level = one(*shards[0])
    for cut in shards[1:]:
        level = level * one(*cut)
    return level


def profile(amount, total, bound, slope):
    loads = [(1 << 20) // math.isqrt(grade ** slope) + 1 for grade in range(2, amount + 1)]
    surplus, holding = total - bound - (amount - 1), [1] * (amount - 1)
    while surplus > 0:
        movable = [i for i in range(amount - 1) if holding[i] < bound]
        whole, budget = sum([loads[i] for i in movable]), surplus
        for i in movable:
            addition = min(bound - holding[i], max(1, budget * loads[i] // whole), surplus)
            holding[i] = holding[i] + addition
            surplus = surplus - addition
    return np.array([bound] + holding)


def ragged(own_key, number_of, total, reach, slope):
    if number_of == 2:
        one = jax.random.randint(own_key, (), max(1, total - reach), min(reach, total - 1) + 1)
        return jnp.stack([one, total - one])
    sizes = jnp.asarray(profile(number_of, total, reach, slope), jnp.int32)
    pairs = (number_of - 1) // 2
    giver, receiver = sizes[1:1 + 2 * pairs:2], sizes[2:2 + 2 * pairs:2]
    slack = jnp.minimum(giver - 1, reach - receiver)
    shifted = jax.random.randint(jax.random.fold_in(own_key, 1), (pairs,), 0, 1 << 20) % (slack + 1)
    sizes = sizes.at[1:1 + 2 * pairs:2].set(giver - shifted).at[2:2 + 2 * pairs:2].set(receiver + shifted)
    return sizes[jax.random.permutation(jax.random.fold_in(own_key, 2), number_of)]


def gaussian(stream_key, shape, scale, bound, shards=(), kind=jnp.bfloat16):
    factor_of = shard_levels(stream_key, shape, shards, -0.22, 0.18) if shards else 1.0
    result = jax.random.normal(stream_key, shape, jnp.float32) * scale * factor_of
    return jnp.minimum(jnp.maximum(result, -bound), bound).astype(kind)


def setup_inputs(seed: int = 0) -> dict:
    splits = jax.random.split(jax.random.key(seed), 8)
    return {
        "resid": draw_resid(jax.random.fold_in(splits[7], 71), 0),
        "pending": gaussian(splits[1], (SECTIONS, TOKENS, D), 1.0, 6.0, ((0, 8), (1, 32))),
        "doc_ids": jax.vmap(lambda own: jnp.searchsorted(jnp.cumsum(ragged(own, DOCS, TOKENS, TOKENS // 2, 0)), jnp.arange(TOKENS), side="right"))(jax.random.split(splits[2], SECTIONS)).reshape((SECTIONS, TOKENS)).astype(jnp.int32),
        "norm_gain": jnp.clip(1.0 + 0.15 * jax.random.normal(splits[3], (SECTIONS, D), jnp.float32), 0.25, 1.75).astype(jnp.bfloat16),
        "q_weight": draw_q_weight(jax.random.fold_in(splits[7], 71), 0),
        "kv_weight": draw_kv_weight(jax.random.fold_in(splits[7], 71), 0),
        "o_weight": gaussian(splits[6], (SECTIONS, HEADS * HD, D), (HEADS * HD // 16) ** -0.5, 0.25, ((0, 8), (1, 32))),
    }


def rms_normed(stream, gain):
    values = stream.astype(jnp.float32)
    mean_square = lax.optimization_barrier(jnp.mean(values * values, axis=-1, keepdims=True))
    return (values * lax.rsqrt(mean_square + 1e-05) * gain.astype(jnp.float32)).astype(jnp.bfloat16)

def doc_mask(documents):
    order = jnp.arange(documents.shape[0], dtype=jnp.int32)
    return (order[:, None] >= order[None, :]) & (documents[:, None] == documents[None, :])

def attend(query_heads, keys, values, mask):
    scores = jnp.einsum('thd,sd->hts', query_heads.astype(jnp.float32), keys.astype(jnp.float32)) / math.sqrt(keys.shape[1])
    probs = jax.nn.softmax(jnp.where(mask[None], scores, -1e+30), axis=-1).astype(jnp.bfloat16)
    context = jnp.einsum('hts,sd->thd', probs.astype(jnp.float32), values.astype(jnp.float32)).astype(jnp.bfloat16)
    return context.reshape(context.shape[0], context.shape[1] * context.shape[2])

def reference(resid, pending, doc_ids, norm_gain, q_weight, kv_weight, o_weight):
    per_block = HEADS // N_TP
    group = HEADS // KV_HEADS

    def one_section(section_args):
        stream, waiting, gain, w_query, w_keyval, w_out, documents = section_args
        normed = rms_normed(stream, gain)
        queries = jnp.dot(normed, w_query, preferred_element_type=jnp.float32).astype(jnp.bfloat16)
        keyvals = jnp.dot(normed, w_keyval, preferred_element_type=jnp.float32).astype(jnp.bfloat16)
        mask = doc_mask(documents)
        token_count = stream.shape[0]

        def block(total, index):
            first_head = (index * per_block).astype(jnp.int32)
            kv_head = (first_head // group).astype(jnp.int32)
            query_heads = lax.dynamic_slice_in_dim(queries, first_head * HD, per_block * HD, 1)
            query_heads = query_heads.reshape(token_count, per_block, HD)
            keys = lax.dynamic_slice_in_dim(keyvals, kv_head * HD, HD, 1)
            values = lax.dynamic_slice_in_dim(keyvals, KV_HEADS * HD + kv_head * HD, HD, 1)
            context = attend(query_heads, keys, values, mask)
            w_rows = lax.dynamic_slice_in_dim(w_out, first_head * HD, per_block * HD, 0)
            term = jnp.dot(context, w_rows, preferred_element_type=jnp.float32).astype(jnp.bfloat16)
            term = lax.optimization_barrier(term)
            return (total + term.astype(jnp.float32), None)
        total, _ = lax.scan(block, jnp.zeros((token_count, D), jnp.float32), jnp.arange(N_TP, dtype=jnp.int32))
        carried = (stream.astype(jnp.float32) + waiting.astype(jnp.float32)).astype(jnp.bfloat16)
        return (carried, total.astype(jnp.bfloat16))
    carried_all, output_all = lax.map(one_section, (resid, pending, norm_gain, q_weight, kv_weight, o_weight, doc_ids))
    return (jnp.roll(carried_all, 1, axis=0), jnp.roll(output_all, 1, axis=0))
```

```python
import functools
import math

import jax
import jax.numpy as jnp
from jax import lax
from jax.experimental import pallas as pl
from jax.experimental.pallas import tpu as pltpu
from jax.sharding import PartitionSpec as P

D = 8192
HD = 128
Z = 8
ROWS = 16
TOK = 256
NC = 4
KC = D // NC
AG_OFF = (0, 0, 1, 2)
RS_OFF = (0, 1, 2, 3)
MESH = pl.DeviceIdType.MESH
F32 = jnp.float32
BF16 = jnp.bfloat16
SAME, OTHER = 0, 1
ZP, ZM, YY = 0, 1, 2

YE = {4: 0, 3: 1, -3: 2, 2: 3, -2: 4}
RP = {3: 5, 2: 6, 1: 7, 0: 8}
RM = {-3: 9, -2: 10, -1: 11, 0: 12}
QP = {1: 13, 0: 14}
QM = {-1: 15, 0: 16}
RY = 17
SLOTS = 18


def kernel(
    resid, pending, doc_ids, gain, wq_hbm, wkv_hbm, wo_hbm,
    next_resid, next_output,
    xg, wq, wkv, wo, accq, acckv, kvs, kvr, ctx, part, rsb, carr,
    ag_s, ag_r, rs_s, rs_r, kv_s, kv_r, lw, ws, wr, sh_s, sh_r,
):
    sec = lax.axis_index("section")
    t = lax.axis_index("tp")
    z, yh, c = t // 4, (t // 2) % 2, t % 2

    def at(zz, yy, cc):
        return (sec, (zz * 2 + yy) * 2 + cc)

    neighbour = (
        at((z + 1) % Z, yh, c),
        at((z + Z - 1) % Z, yh, c),
        at(z, 1 - yh, c),
    )
    sibling = at(z, yh, 1 - c)
    next_sec = ((sec + 1) % 8, t)
    prev_sec = ((sec + 7) % 8, t)

    def block(kind, d):
        b = ((z + d + Z) % Z) * 2 + (yh if kind == SAME else 1 - yh)
        return pl.ds(pl.multiple_of(b * ROWS, ROWS), ROWS)

    barrier = pltpu.get_barrier_semaphore()
    for o in range(1, 32):
        pl.semaphore_signal(barrier, inc=1, device_id=(sec, (t + o) % 32), device_id_type=MESH)
    for dev in (next_sec, prev_sec):
        pl.semaphore_signal(barrier, inc=1, device_id=dev, device_id_type=MESH)

    def cols(j):
        return pl.ds(j * KC, KC)

    pieces = [(wkv_hbm, wkv.at[pl.ds(pl.multiple_of(c * 32, 32), 32)])]
    for j in range(NC):
        pieces.append((wq_hbm.at[cols(j)], wq.at[c, cols(j)]))
    for j in range(NC):
        pieces.append(
            (wo_hbm.at[:, cols(j)], wo.at[pl.ds(pl.multiple_of(c * 256, 256), 256), cols(j)])
        )
    local = [pltpu.make_async_copy(s, d, lw.at[i]) for i, (s, d) in enumerate(pieces)]
    far = [
        pltpu.make_async_remote_copy(
            src_ref=s, dst_ref=d, send_sem=ws.at[i], recv_sem=wr.at[i],
            device_id=sibling, device_id_type=MESH,
        )
        for i, (s, d) in enumerate(pieces)
    ]
    for copy in local:
        copy.start()

    stream = resid[...].astype(F32)
    scale = lax.rsqrt(jnp.mean(stream * stream, axis=-1, keepdims=True) + 1e-05)
    for j in range(NC):
        piece = resid[:, j * KC : (j + 1) * KC].astype(F32)
        xg[j, block(SAME, 0)] = (
            piece * scale * gain[:, j * KC : (j + 1) * KC].astype(F32)
        ).astype(BF16)

    pl.semaphore_wait(barrier, 33)

    sends = []

    count = [0] * NC

    def ag_send(j, kind, d, way):
        dd = d - 1 if way == ZP else d + 1 if way == ZM else d
        kk = kind if way != YY else 1 - kind
        ref = xg.at[j, block(kind, d)]
        copy = pltpu.make_async_remote_copy(
            src_ref=ref, dst_ref=ref,
            send_sem=ag_s.at[j * 16 + count[j]], recv_sem=ag_r.at[j * 16 + kk * 8 + dd % 8],
            device_id=neighbour[way], device_id_type=MESH,
        )
        count[j] += 1
        copy.start()
        sends.append(copy)

    def ag_wait(j, kind, d):
        ref = xg.at[j, block(kind, d)]
        pltpu.make_async_remote_copy(
            src_ref=ref, dst_ref=ref,
            send_sem=ag_s.at[j * 16], recv_sem=ag_r.at[j * 16 + kind * 8 + d % 8],
            device_id=neighbour[YY], device_id_type=MESH,
        ).wait_recv()

    def ag_step(j, step):
        even = j % 2 == 0
        if step == 0:
            ag_send(j, SAME, 0, ZP)
            ag_send(j, SAME, 0, ZM)
            ag_send(j, SAME, 0, YY)
        elif step == 1:
            ag_wait(j, SAME, -1)
            ag_send(j, SAME, -1, ZP)
            ag_wait(j, SAME, 1)
            ag_send(j, SAME, 1, ZM)
            ag_wait(j, OTHER, 0)
            ag_send(j, OTHER, 0, ZP)
            ag_send(j, OTHER, 0, ZM)
        elif step == 2:
            ag_wait(j, SAME, -2)
            ag_send(j, SAME, -2, ZP)
            if not even:
                ag_send(j, SAME, -2, YY)
            ag_wait(j, SAME, 2)
            ag_send(j, SAME, 2, ZM)
            if not even:
                ag_send(j, SAME, 2, YY)
            ag_wait(j, OTHER, -1)
            ag_wait(j, OTHER, 1)
            if even:
                ag_send(j, OTHER, -1, ZP)
                ag_send(j, OTHER, 1, ZM)
        elif step == 3:
            ag_wait(j, SAME, -3)
            if even:
                ag_send(j, SAME, -3, ZP)
            ag_send(j, SAME, -3, YY)
            ag_wait(j, SAME, 3)
            if not even:
                ag_send(j, SAME, 3, ZM)
            ag_send(j, SAME, 3, YY)
        elif step == 4:
            ag_wait(j, SAME, 4)
            ag_send(j, SAME, 4, YY)
        elif step == 5:
            for d in (-2, 2, -3, 3, 4):
                ag_wait(j, OTHER, d)

    def weight_ready(i):
        local[i].wait()
        far[i].wait_recv()

    def project_kv(j):
        if j == 0:
            weight_ready(0)
        term = lax.dot_general(
            wkv[:, j * KC : (j + 1) * KC], xg[j], (((1,), (1,)), ((), ())),
            preferred_element_type=F32,
        )
        acckv[...] = term if j == 0 else acckv[...] + term

    def project_q(j):
        weight_ready(1 + j)
        for cc in range(2):
            term = jnp.dot(
                xg[j], wq[cc, j * KC : (j + 1) * KC, :], preferred_element_type=F32
            )
            span = slice(cc * 256, (cc + 1) * 256)
            accq[:, span] = term if j == 0 else accq[:, span] + term

    for r in range(max(AG_OFF) + 6):
        for j in range(NC):
            step = r - AG_OFF[j]
            if 0 <= step <= 5:
                ag_step(j, step)
        if r == 0:
            for copy in far:
                copy.start()
        for j in range(NC - 1):
            if r - AG_OFF[j] == 5:
                project_kv(j)
                project_q(j)

    project_kv(NC - 1)
    kvs[...] = acckv[...].astype(BF16)
    kv_rows = pl.ds(pl.multiple_of((z // 4) * 128 + yh * 64, 64), 64)
    kv_index = (z // 4) * 4 + yh * 2 + c
    kv_copies = []
    for n in range(8):
        zz, yy, cc = 2 * (z % 4) + n // 4, (n // 2) % 2, n % 2
        mine = (zz == z) & (yy == yh) & (cc == c)
        copy = pltpu.make_async_remote_copy(
            src_ref=kvs, dst_ref=kvr.at[c, kv_rows],
            send_sem=kv_s.at[n], recv_sem=kv_r.at[kv_index],
            device_id=at(zz, yy, cc), device_id_type=MESH,
        )
        kv_copies.append((mine, copy))

        @pl.when(mine)
        def _():
            pltpu.make_async_copy(kvs, kvr.at[c, kv_rows], kv_r.at[kv_index]).start()

        @pl.when(jnp.logical_not(mine))
        def _(copy=copy):
            copy.start()

    carr[...] = (resid[...].astype(F32) + pending[...].astype(F32)).astype(BF16)
    carry = pltpu.make_async_remote_copy(
        src_ref=carr, dst_ref=next_resid,
        send_sem=sh_s.at[NC], recv_sem=sh_r.at[NC],
        device_id=next_sec, device_id_type=MESH,
    )
    carry.start()

    project_q(NC - 1)

    docs = doc_ids[...].astype(F32)
    row = lax.broadcasted_iota(jnp.int32, (TOK, 1), 0)
    mine_at = ((row // 16) * 32 + c * 16 + row % 16).astype(F32)
    key = lax.broadcasted_iota(jnp.int32, (1, 2 * TOK), 1)
    key_at = (((key % TOK) // 16) * 32 + (key // TOK) * 16 + key % 16).astype(F32)
    first = jnp.zeros((TOK, 1), F32)
    for k in range(1, 4):
        begin = jnp.sum(jnp.where(docs < k, 1.0, 0.0), axis=-1, keepdims=True)
        first = jnp.maximum(first, jnp.where(mine_at >= begin, begin, 0.0))
    mask = (key_at <= mine_at) & (key_at >= first)

    for i in range(8):
        ref = kvr.at[i % 2, pl.ds((i // 2) * 64, 64)]
        pltpu.make_async_remote_copy(
            src_ref=ref, dst_ref=ref, send_sem=kv_s.at[0], recv_sem=kv_r.at[i],
            device_id=sibling, device_id_type=MESH,
        ).wait_recv()

    keys = jnp.concatenate([kvr[0, :128, :], kvr[1, :128, :]], axis=1)
    values = jnp.concatenate([kvr[0, 128:, :], kvr[1, 128:, :]], axis=1)
    for h in range(4):
        query = accq[:, h * HD : (h + 1) * HD].astype(BF16)
        scores = jnp.dot(query, keys, preferred_element_type=F32) / math.sqrt(HD)
        scores = jnp.where(mask, scores, -1e30)
        top = jnp.max(scores, axis=-1, keepdims=True)
        weight = jnp.exp(scores - top)
        probs = (weight / jnp.sum(weight, axis=-1, keepdims=True)).astype(BF16)
        ctx[:, h * HD : (h + 1) * HD] = lax.dot_general(
            probs, values, (((1,), (1,)), ((), ())), preferred_element_type=F32
        ).astype(BF16)

    sent = [0] * NC

    def rs_send(j, kind, d, way, slot):
        copy = pltpu.make_async_remote_copy(
            src_ref=part.at[j, block(kind, d)], dst_ref=rsb.at[j, slot],
            send_sem=rs_s.at[j * 20 + sent[j]], recv_sem=rs_r.at[j * SLOTS + slot],
            device_id=neighbour[way], device_id_type=MESH,
        )
        sent[j] += 1
        copy.start()
        sends.append(copy)

    def rs_add(j, kind, d, slots):
        for slot in slots:
            ref = rsb.at[j, slot]
            pltpu.make_async_remote_copy(
                src_ref=ref, dst_ref=ref,
                send_sem=rs_s.at[j * 20], recv_sem=rs_r.at[j * SLOTS + slot],
                device_id=neighbour[YY], device_id_type=MESH,
            ).wait_recv()
        total = part[j, block(kind, d)].astype(F32)
        for slot in slots:
            total = total + rsb[j, slot].astype(F32)
        part[j, block(kind, d)] = total.astype(BF16)

    ships = []

    def rs_step(j, step):
        even = j % 2 == 0
        if step == 0:
            weight_ready(1 + NC + j)
            for n in range(0, KC, 512):
                part[j, :, n : n + 512] = jnp.dot(
                    ctx[...], wo[:, j * KC + n : j * KC + n + 512], preferred_element_type=F32
                ).astype(BF16)
            rs_send(j, OTHER, 4, YY, YE[4])
            if even:
                rs_send(j, OTHER, 2, ZP, QP[1])
                rs_send(j, OTHER, -2, ZM, QM[-1])
            else:
                rs_send(j, OTHER, 1, ZP, QP[0])
                rs_send(j, OTHER, -1, ZM, QM[0])
            rs_send(j, OTHER, 3, YY, YE[3])
            rs_send(j, OTHER, -3, YY, YE[-3])
            if not even:
                rs_send(j, OTHER, 2, YY, YE[2])
                rs_send(j, OTHER, -2, YY, YE[-2])
        elif step == 1:
            rs_add(j, SAME, 4, [YE[4]])
            if even:
                rs_send(j, SAME, 4, ZP, RP[3])
                rs_add(j, OTHER, 1, [QP[1]])
                rs_send(j, OTHER, 1, ZP, QP[0])
                rs_add(j, OTHER, -1, [QM[-1]])
                rs_send(j, OTHER, -1, ZM, QM[0])
            else:
                rs_send(j, SAME, 4, ZM, RM[-3])
                rs_add(j, OTHER, 0, [QP[0], QM[0]])
                rs_send(j, OTHER, 0, YY, RY)
        elif step == 2:
            if even:
                rs_add(j, SAME, -3, [YE[-3]])
                rs_send(j, SAME, -3, ZM, RM[-2])
                rs_add(j, SAME, 3, [YE[3], RP[3]])
                rs_send(j, SAME, 3, ZP, RP[2])
                rs_add(j, OTHER, 0, [QP[0], QM[0]])
                rs_send(j, OTHER, 0, YY, RY)
            else:
                rs_add(j, SAME, 3, [YE[3]])
                rs_send(j, SAME, 3, ZP, RP[2])
                rs_add(j, SAME, -3, [YE[-3], RM[-3]])
                rs_send(j, SAME, -3, ZM, RM[-2])
        elif step == 3:
            rs_add(j, SAME, 2, [RP[2]] if even else [RP[2], YE[2]])
            rs_send(j, SAME, 2, ZP, RP[1])
            rs_add(j, SAME, -2, [RM[-2]] if even else [RM[-2], YE[-2]])
            rs_send(j, SAME, -2, ZM, RM[-1])
        elif step == 4:
            rs_add(j, SAME, 1, [RP[1]])
            rs_send(j, SAME, 1, ZP, RP[0])
            rs_add(j, SAME, -1, [RM[-1]])
            rs_send(j, SAME, -1, ZM, RM[0])
        elif step == 5:
            rs_add(j, SAME, 0, [RP[0], RM[0], RY])
            ship = pltpu.make_async_remote_copy(
                src_ref=part.at[j, block(SAME, 0)], dst_ref=next_output.at[:, cols(j)],
                send_sem=sh_s.at[j], recv_sem=sh_r.at[j],
                device_id=next_sec, device_id_type=MESH,
            )
            ship.start()
            ships.append(ship)

    for r in range(max(RS_OFF) + 6):
        for j in range(NC):
            step = r - RS_OFF[j]
            if 0 <= step <= 5:
                rs_step(j, step)

    for copy in sends:
        copy.wait_send()
    for copy in far:
        copy.wait_send()
    for mine, copy in kv_copies:

        @pl.when(jnp.logical_not(mine))
        def _(copy=copy):
            copy.wait_send()

    carry.wait()
    for ship in ships:
        ship.wait()


def body(resid, pending, doc_ids, norm_gain, q_weight, kv_weight, o_weight):
    vmem = pl.BlockSpec(memory_space=pltpu.VMEM)
    hbm = pl.BlockSpec(memory_space=pl.ANY)
    dma = pltpu.SemaphoreType.DMA
    out = jax.ShapeDtypeStruct((ROWS, D), BF16)
    next_resid, next_output = pl.pallas_call(
        kernel,
        out_shape=(out, out),
        in_specs=[vmem] * 4 + [hbm] * 3,
        out_specs=(vmem, vmem),
        scratch_shapes=[
            pltpu.VMEM((NC, TOK, KC), BF16),
            pltpu.VMEM((2, D, 256), BF16),
            pltpu.VMEM((64, D), BF16),
            pltpu.VMEM((512, D), BF16),
            pltpu.VMEM((TOK, 512), F32),
            pltpu.VMEM((64, TOK), F32),
            pltpu.VMEM((64, TOK), BF16),
            pltpu.VMEM((2, 256, TOK), BF16),
            pltpu.VMEM((TOK, 512), BF16),
            pltpu.VMEM((NC, TOK, KC), BF16),
            pltpu.VMEM((NC, SLOTS, ROWS, KC), BF16),
            pltpu.VMEM((ROWS, D), BF16),
            dma((NC * 16,)),
            dma((NC * 16,)),
            dma((NC * 20,)),
            dma((NC * SLOTS,)),
            dma((8,)),
            dma((8,)),
            dma((1 + 2 * NC,)),
            dma((1 + 2 * NC,)),
            dma((1 + 2 * NC,)),
            dma((NC + 1,)),
            dma((NC + 1,)),
        ],
        compiler_params=pltpu.CompilerParams(
            collective_id=0, has_side_effects=True, vmem_limit_bytes=56 << 20
        ),
        name="module",
    )(
        resid[0], pending[0], doc_ids, norm_gain,
        q_weight[0], kv_weight[0].T, o_weight[0],
    )
    return next_resid[None], next_output[None]


def solution(mesh):
    in_specs = (
        P("section", "tp", None),
        P("section", "tp", None),
        P("section", None),
        P("section", None),
        P("section", None, "tp"),
        P("section", None, "tp"),
        P("section", "tp", None),
    )
    out_specs = (P("section", "tp", None), P("section", "tp", None))
    return jax.shard_map(body, mesh=mesh, in_specs=in_specs, out_specs=out_specs, check_vma=False)
```

```python
import functools
import math

import jax
import jax.numpy as jnp
from jax import lax
from jax.experimental import pallas as pl
from jax.experimental.pallas import tpu as pltpu
from jax.sharding import PartitionSpec as P

D = 8192
HD = 128
Z = 8
ROWS = 16
TOK = 256
NC = 4
KC = D // NC
AG_LAP = 0.25
AG_LAG = 0.5
AG_MM = 0.5
RS_LAP = 0.25
MESH = pl.DeviceIdType.MESH
F32 = jnp.float32
BF16 = jnp.bfloat16
SAME, OTHER = 0, 1
ZP, ZM, YY = 0, 1, 2

YE = {4: 0, 3: 1, 2: 2, 1: 3}
RF = {3: 4, 2: 5, 1: 6, 0: 7}
RB = {2: 8, 1: 9, 0: 10}
QB = {2: 11, 1: 12, 0: 13}
RY = 14
SLOTS = 15


def kernel(
    resid, pending, doc_ids, gain, wq_hbm, wkv_hbm, wo_hbm,
    next_resid, next_output,
    xg, wq, wkv, wo, accq, acckv, kvs, kvr, ctx, part, rsb, carr,
    ag_s, ag_r, rs_s, rs_r, kv_s, kv_r, lw, ws, wr, sh_s, sh_r,
):
    sec = lax.axis_index("section")
    t = lax.axis_index("tp")
    z, yh, c = t // 4, (t // 2) % 2, t % 2

    def at(zz, yy, cc):
        return (sec, (zz * 2 + yy) * 2 + cc)

    neighbour = (
        at((z + 1) % Z, yh, c),
        at((z + Z - 1) % Z, yh, c),
        at(z, 1 - yh, c),
    )
    sibling = at(z, yh, 1 - c)
    next_sec = ((sec + 1) % 8, t)
    prev_sec = ((sec + 7) % 8, t)

    def block(kind, d):
        b = ((z + d + Z) % Z) * 2 + (yh if kind == SAME else 1 - yh)
        return pl.ds(pl.multiple_of(b * ROWS, ROWS), ROWS)

    barrier = pltpu.get_barrier_semaphore()
    for o in range(1, 32):
        pl.semaphore_signal(barrier, inc=1, device_id=(sec, (t + o) % 32), device_id_type=MESH)
    for dev in (next_sec, prev_sec):
        pl.semaphore_signal(barrier, inc=1, device_id=dev, device_id_type=MESH)

    def cols(j):
        return pl.ds(j * KC, KC)

    pieces = [(wkv_hbm, wkv.at[pl.ds(pl.multiple_of(c * 32, 32), 32)])]
    for j in range(NC):
        pieces.append((wq_hbm.at[cols(j)], wq.at[c, cols(j)]))
    for j in range(NC):
        pieces.append(
            (wo_hbm.at[:, cols(j)], wo.at[pl.ds(pl.multiple_of(c * 256, 256), 256), cols(j)])
        )
    local = [pltpu.make_async_copy(s, d, lw.at[i]) for i, (s, d) in enumerate(pieces)]
    far = [
        pltpu.make_async_remote_copy(
            src_ref=s, dst_ref=d, send_sem=ws.at[i], recv_sem=wr.at[i],
            device_id=sibling, device_id_type=MESH,
        )
        for i, (s, d) in enumerate(pieces)
    ]
    for copy in local:
        copy.start()

    stream = resid[...].astype(F32)
    scale = lax.rsqrt(jnp.mean(stream * stream, axis=-1, keepdims=True) + 1e-05)
    for j in range(NC):
        piece = resid[:, j * KC : (j + 1) * KC].astype(F32)
        xg[j, block(SAME, 0)] = (
            piece * scale * gain[:, j * KC : (j + 1) * KC].astype(F32)
        ).astype(BF16)

    pl.semaphore_wait(barrier, 33)

    sends = []

    count = [0] * NC

    def ag_send(j, kind, d, way):
        dd = d - 1 if way == ZP else d + 1 if way == ZM else d
        kk = kind if way != YY else 1 - kind
        ref = xg.at[j, block(kind, d)]
        copy = pltpu.make_async_remote_copy(
            src_ref=ref, dst_ref=ref,
            send_sem=ag_s.at[j * 16 + count[j]], recv_sem=ag_r.at[j * 16 + kk * 8 + dd % 8],
            device_id=neighbour[way], device_id_type=MESH,
        )
        count[j] += 1
        copy.start()
        sends.append(copy)

    def ag_wait(j, kind, d):
        ref = xg.at[j, block(kind, d)]
        pltpu.make_async_remote_copy(
            src_ref=ref, dst_ref=ref,
            send_sem=ag_s.at[j * 16], recv_sem=ag_r.at[j * 16 + kind * 8 + d % 8],
            device_id=neighbour[YY], device_id_type=MESH,
        ).wait_recv()

    def ag_actions(j):
        e = 1 if j % 2 == 0 else -1
        fore, back = (ZP, ZM) if e == 1 else (ZM, ZP)

        def begin():
            for way in (back, fore, YY):
                ag_send(j, SAME, 0, way)

        def relay(kind, d, *ways):
            def act():
                ag_wait(j, kind, d)
                for way in ways:
                    ag_send(j, kind, d, way)

            return act

        def finish():
            for kind, d in ((SAME, -3), (OTHER, 1), (OTHER, 2), (OTHER, 3), (OTHER, -3), (OTHER, 4)):
                ag_wait(j, kind, d * e if d != 4 else 4)

        return [
            (0, begin),
            (1, relay(SAME, e, back, YY)),
            (1, relay(SAME, -e, fore)),
            (1 + AG_LAG, relay(OTHER, 0, fore)),
            (2, relay(SAME, 2 * e, back, YY)),
            (2, relay(SAME, -2 * e, fore)),
            (2 + AG_LAG, relay(OTHER, -e, fore)),
            (3, relay(SAME, 3 * e, back, YY)),
            (3 + AG_LAG, relay(OTHER, -2 * e, fore)),
            (4, relay(SAME, 4, YY)),
            (5, finish),
        ]

    def weight_ready(i):
        local[i].wait()
        far[i].wait_recv()

    def project_kv(j):
        if j == 0:
            weight_ready(0)
        term = lax.dot_general(
            wkv[:, j * KC : (j + 1) * KC], xg[j], (((1,), (1,)), ((), ())),
            preferred_element_type=F32,
        )
        acckv[...] = term if j == 0 else acckv[...] + term

    def project_q(j):
        weight_ready(1 + j)
        for cc in range(2):
            term = jnp.dot(
                xg[j], wq[cc, j * KC : (j + 1) * KC, :], preferred_element_type=F32
            )
            span = slice(cc * 256, (cc + 1) * 256)
            accq[:, span] = term if j == 0 else accq[:, span] + term

    def send_weights():
        for copy in far:
            copy.start()

    def project(j):
        def act():
            project_kv(j)
            project_q(j)

        return act

    actions = [(0, send_weights)]
    for j in range(NC):
        actions += [(j * AG_LAP + when, act) for when, act in ag_actions(j)]
        if j < NC - 1:
            actions.append((j * AG_LAP + 5 + AG_MM, project(j)))
    for _, act in sorted(actions, key=lambda item: item[0]):
        act()

    project_kv(NC - 1)
    kvs[...] = acckv[...].astype(BF16)
    kv_rows = pl.ds(pl.multiple_of((z // 4) * 128 + yh * 64, 64), 64)
    kv_index = (z // 4) * 4 + yh * 2 + c
    kv_copies = []
    for n in range(8):
        zz, yy, cc = 2 * (z % 4) + n // 4, (n // 2) % 2, n % 2
        mine = (zz == z) & (yy == yh) & (cc == c)
        copy = pltpu.make_async_remote_copy(
            src_ref=kvs, dst_ref=kvr.at[c, kv_rows],
            send_sem=kv_s.at[n], recv_sem=kv_r.at[kv_index],
            device_id=at(zz, yy, cc), device_id_type=MESH,
        )
        kv_copies.append((mine, copy))

        @pl.when(mine)
        def _():
            pltpu.make_async_copy(kvs, kvr.at[c, kv_rows], kv_r.at[kv_index]).start()

        @pl.when(jnp.logical_not(mine))
        def _(copy=copy):
            copy.start()

    carr[...] = (resid[...].astype(F32) + pending[...].astype(F32)).astype(BF16)
    carry = pltpu.make_async_remote_copy(
        src_ref=carr, dst_ref=next_resid,
        send_sem=sh_s.at[NC], recv_sem=sh_r.at[NC],
        device_id=next_sec, device_id_type=MESH,
    )
    carry.start()

    project_q(NC - 1)

    docs = doc_ids[...].astype(F32)
    row = lax.broadcasted_iota(jnp.int32, (TOK, 1), 0)
    mine_at = ((row // 16) * 32 + c * 16 + row % 16).astype(F32)
    key = lax.broadcasted_iota(jnp.int32, (1, 2 * TOK), 1)
    key_at = (((key % TOK) // 16) * 32 + (key // TOK) * 16 + key % 16).astype(F32)
    first = jnp.zeros((TOK, 1), F32)
    for k in range(1, 4):
        begin = jnp.sum(jnp.where(docs < k, 1.0, 0.0), axis=-1, keepdims=True)
        first = jnp.maximum(first, jnp.where(mine_at >= begin, begin, 0.0))
    mask = (key_at <= mine_at) & (key_at >= first)

    for i in range(8):
        ref = kvr.at[i % 2, pl.ds((i // 2) * 64, 64)]
        pltpu.make_async_remote_copy(
            src_ref=ref, dst_ref=ref, send_sem=kv_s.at[0], recv_sem=kv_r.at[i],
            device_id=sibling, device_id_type=MESH,
        ).wait_recv()

    keys = jnp.concatenate([kvr[0, :128, :], kvr[1, :128, :]], axis=1)
    values = jnp.concatenate([kvr[0, 128:, :], kvr[1, 128:, :]], axis=1)
    for h in range(4):
        query = accq[:, h * HD : (h + 1) * HD].astype(BF16)
        scores = jnp.dot(query, keys, preferred_element_type=F32) / math.sqrt(HD)
        scores = jnp.where(mask, scores, -1e30)
        top = jnp.max(scores, axis=-1, keepdims=True)
        weight = jnp.exp(scores - top)
        probs = (weight / jnp.sum(weight, axis=-1, keepdims=True)).astype(BF16)
        ctx[:, h * HD : (h + 1) * HD] = lax.dot_general(
            probs, values, (((1,), (1,)), ((), ())), preferred_element_type=F32
        ).astype(BF16)

    sent = [0] * NC

    def rs_send(j, kind, d, way, slot):
        copy = pltpu.make_async_remote_copy(
            src_ref=part.at[j, block(kind, d)], dst_ref=rsb.at[j, slot],
            send_sem=rs_s.at[j * 20 + sent[j]], recv_sem=rs_r.at[j * SLOTS + slot],
            device_id=neighbour[way], device_id_type=MESH,
        )
        sent[j] += 1
        copy.start()
        sends.append(copy)

    def rs_add(j, kind, d, slots):
        for slot in slots:
            ref = rsb.at[j, slot]
            pltpu.make_async_remote_copy(
                src_ref=ref, dst_ref=ref,
                send_sem=rs_s.at[j * 20], recv_sem=rs_r.at[j * SLOTS + slot],
                device_id=neighbour[YY], device_id_type=MESH,
            ).wait_recv()
        total = part[j, block(kind, d)].astype(F32)
        for slot in slots:
            total = total + rsb[j, slot].astype(F32)
        part[j, block(kind, d)] = total.astype(BF16)

    ships = []

    def rs_actions(j):
        e = 1 if j % 2 == 0 else -1
        fore, back = (ZP, ZM) if e == 1 else (ZM, ZP)

        def begin():
            weight_ready(1 + NC + j)
            for n in range(0, KC, 512):
                part[j, :, n : n + 512] = jnp.dot(
                    ctx[...], wo[:, j * KC + n : j * KC + n + 512], preferred_element_type=F32
                ).astype(BF16)
            rs_send(j, OTHER, 4, YY, YE[4])
            rs_send(j, OTHER, -3 * e, back, QB[2])
            rs_send(j, OTHER, 3 * e, YY, YE[3])
            rs_send(j, SAME, -3 * e, back, RB[2])
            rs_send(j, OTHER, 2 * e, YY, YE[2])
            rs_send(j, OTHER, e, YY, YE[1])

        def relay(kind, d, slots, way, slot):
            def act():
                rs_add(j, kind, d, slots)
                rs_send(j, kind, d, way, slot)

            return act

        def finish():
            rs_add(j, SAME, 0, [RF[0], RB[0], RY])
            ship = pltpu.make_async_remote_copy(
                src_ref=part.at[j, block(SAME, 0)], dst_ref=next_output.at[:, cols(j)],
                send_sem=sh_s.at[j], recv_sem=sh_r.at[j],
                device_id=next_sec, device_id_type=MESH,
            )
            ship.start()
            ships.append(ship)

        return [
            (0, begin),
            (1, relay(SAME, 4, [YE[4]], fore, RF[3])),
            (1, relay(OTHER, -2 * e, [QB[2]], back, QB[1])),
            (1, relay(SAME, -2 * e, [RB[2]], back, RB[1])),
            (2, relay(SAME, 3 * e, [YE[3], RF[3]], fore, RF[2])),
            (2, relay(OTHER, -e, [QB[1]], back, QB[0])),
            (2, relay(SAME, -e, [RB[1]], back, RB[0])),
            (3, relay(SAME, 2 * e, [YE[2], RF[2]], fore, RF[1])),
            (3, relay(OTHER, 0, [QB[0]], YY, RY)),
            (4, relay(SAME, e, [YE[1], RF[1]], fore, RF[0])),
            (5, finish),
        ]

    actions = []
    for j in range(NC):
        actions += [(j * RS_LAP + when, act) for when, act in rs_actions(j)]
    for _, act in sorted(actions, key=lambda item: item[0]):
        act()

    for copy in sends:
        copy.wait_send()
    for copy in far:
        copy.wait_send()
    for mine, copy in kv_copies:

        @pl.when(jnp.logical_not(mine))
        def _(copy=copy):
            copy.wait_send()

    carry.wait()
    for ship in ships:
        ship.wait()


def body(resid, pending, doc_ids, norm_gain, q_weight, kv_weight, o_weight):
    vmem = pl.BlockSpec(memory_space=pltpu.VMEM)
    hbm = pl.BlockSpec(memory_space=pl.ANY)
    dma = pltpu.SemaphoreType.DMA
    out = jax.ShapeDtypeStruct((ROWS, D), BF16)
    next_resid, next_output = pl.pallas_call(
        kernel,
        out_shape=(out, out),
        in_specs=[vmem] * 4 + [hbm] * 3,
        out_specs=(vmem, vmem),
        scratch_shapes=[
            pltpu.VMEM((NC, TOK, KC), BF16),
            pltpu.VMEM((2, D, 256), BF16),
            pltpu.VMEM((64, D), BF16),
            pltpu.VMEM((512, D), BF16),
            pltpu.VMEM((TOK, 512), F32),
            pltpu.VMEM((64, TOK), F32),
            pltpu.VMEM((64, TOK), BF16),
            pltpu.VMEM((2, 256, TOK), BF16),
            pltpu.VMEM((TOK, 512), BF16),
            pltpu.VMEM((NC, TOK, KC), BF16),
            pltpu.VMEM((NC, SLOTS, ROWS, KC), BF16),
            pltpu.VMEM((ROWS, D), BF16),
            dma((NC * 16,)),
            dma((NC * 16,)),
            dma((NC * 20,)),
            dma((NC * SLOTS,)),
            dma((8,)),
            dma((8,)),
            dma((1 + 2 * NC,)),
            dma((1 + 2 * NC,)),
            dma((1 + 2 * NC,)),
            dma((NC + 1,)),
            dma((NC + 1,)),
        ],
        compiler_params=pltpu.CompilerParams(
            collective_id=0, has_side_effects=True, vmem_limit_bytes=56 << 20
        ),
        name="module",
    )(
        resid[0], pending[0], doc_ids, norm_gain,
        q_weight[0], kv_weight[0].T, o_weight[0],
    )
    return next_resid[None], next_output[None]


def solution(mesh):
    in_specs = (
        P("section", "tp", None),
        P("section", "tp", None),
        P("section", None),
        P("section", None),
        P("section", None, "tp"),
        P("section", None, "tp"),
        P("section", "tp", None),
    )
    out_specs = (P("section", "tp", None), P("section", "tp", None))
    return jax.shard_map(body, mesh=mesh, in_specs=in_specs, out_specs=out_specs, check_vma=False)
```

```python
import functools
import math

import jax
import jax.numpy as jnp
from jax import lax
from jax.experimental import pallas as pl
from jax.experimental.pallas import tpu as pltpu
from jax.sharding import PartitionSpec as P

D = 8192
HD = 128
Z = 8
ROWS = 16
TOK = 256
NC = 4
KC = D // NC
VMEM = 56
FINISH = 1
AG_LAP = 0.25
AG_LAG = 1.5
AG_MM = 0.5
RS_LAP = 0
RS_Y = (0.1, 0.2, 0.3)
CARRY = 5.12
MESH = pl.DeviceIdType.MESH
F32 = jnp.float32
BF16 = jnp.bfloat16
SAME, OTHER = 0, 1
ZP, ZM, YY = 0, 1, 2

YE = {4: 0, 3: 1, 2: 2, 1: 3}
RF = {3: 4, 2: 5, 1: 6, 0: 7}
RB = {2: 8, 1: 9, 0: 10}
QB = {2: 11, 1: 12, 0: 13}
SLOTS = 14


def kernel(
    resid, pending, doc_ids, gain, wq_hbm, wkv_hbm, wo_hbm,
    next_resid, fin,
    xg, wq, wkv, wo, accq, acckv, kvs, kvr, ctx, part, rsb, carr,
    ag_s, ag_r, rs_s, rs_r, kv_s, kv_r, lw, ws, wr, sh_s, sh_r, fin_s, fin_r,
):
    sec = lax.axis_index("section")
    t = lax.axis_index("tp")
    z, yh, c = t // 4, (t // 2) % 2, t % 2

    def at(zz, yy, cc):
        return (sec, (zz * 2 + yy) * 2 + cc)

    neighbour = (
        at((z + 1) % Z, yh, c),
        at((z + Z - 1) % Z, yh, c),
        at(z, 1 - yh, c),
    )
    sibling = at(z, yh, 1 - c)
    across = (z * 2 + 1 - yh) * 2 + c
    after, before = (sec + 1) % 8, (sec + 7) % 8
    heirs = ((after, t), (after, across))

    def block(kind, d):
        b = ((z + d + Z) % Z) * 2 + (yh if kind == SAME else 1 - yh)
        return pl.ds(pl.multiple_of(b * ROWS, ROWS), ROWS)

    barrier = pltpu.get_barrier_semaphore()
    for o in range(1, 32):
        pl.semaphore_signal(barrier, inc=1, device_id=(sec, (t + o) % 32), device_id_type=MESH)
    for dev in (*heirs, (before, t), (before, across)):
        pl.semaphore_signal(barrier, inc=1, device_id=dev, device_id_type=MESH)

    def cols(j):
        return pl.ds(j * KC, KC)

    pieces = [(wkv_hbm, wkv.at[pl.ds(pl.multiple_of(c * 32, 32), 32)])]
    for j in range(NC):
        pieces.append((wq_hbm.at[cols(j)], wq.at[c, cols(j)]))
    for j in range(NC):
        pieces.append(
            (wo_hbm.at[:, cols(j)], wo.at[pl.ds(pl.multiple_of(c * 256, 256), 256), cols(j)])
        )
    local = [pltpu.make_async_copy(s, d, lw.at[i]) for i, (s, d) in enumerate(pieces)]
    far = [
        pltpu.make_async_remote_copy(
            src_ref=s, dst_ref=d, send_sem=ws.at[i], recv_sem=wr.at[i],
            device_id=sibling, device_id_type=MESH,
        )
        for i, (s, d) in enumerate(pieces)
    ]
    for copy in local:
        copy.start()

    stream = resid[...].astype(F32)
    scale = lax.rsqrt(jnp.mean(stream * stream, axis=-1, keepdims=True) + 1e-05)
    for j in range(NC):
        piece = resid[:, j * KC : (j + 1) * KC].astype(F32)
        xg[j, block(SAME, 0)] = (
            piece * scale * gain[:, j * KC : (j + 1) * KC].astype(F32)
        ).astype(BF16)

    pl.semaphore_wait(barrier, 35)

    sends = []

    count = [0] * NC

    def ag_send(j, kind, d, way):
        dd = d - 1 if way == ZP else d + 1 if way == ZM else d
        kk = kind if way != YY else 1 - kind
        ref = xg.at[j, block(kind, d)]
        copy = pltpu.make_async_remote_copy(
            src_ref=ref, dst_ref=ref,
            send_sem=ag_s.at[j * 16 + count[j]], recv_sem=ag_r.at[j * 16 + kk * 8 + dd % 8],
            device_id=neighbour[way], device_id_type=MESH,
        )
        count[j] += 1
        copy.start()
        sends.append(copy)

    def ag_wait(j, kind, d):
        ref = xg.at[j, block(kind, d)]
        pltpu.make_async_remote_copy(
            src_ref=ref, dst_ref=ref,
            send_sem=ag_s.at[j * 16], recv_sem=ag_r.at[j * 16 + kind * 8 + d % 8],
            device_id=neighbour[YY], device_id_type=MESH,
        ).wait_recv()

    def ag_actions(j):
        e = 1 if j % 2 == 0 else -1
        fore, back = (ZP, ZM) if e == 1 else (ZM, ZP)

        def begin():
            for way in (back, fore, YY):
                ag_send(j, SAME, 0, way)

        def relay(kind, d, *ways):
            def act():
                ag_wait(j, kind, d)
                for way in ways:
                    ag_send(j, kind, d, way)

            return act

        def finish():
            for kind, d in ((SAME, -3), (OTHER, 1), (OTHER, 2), (OTHER, 3), (OTHER, -3), (OTHER, 4)):
                ag_wait(j, kind, d * e if d != 4 else 4)

        return [
            (0, begin),
            (1, relay(SAME, e, back, YY)),
            (1, relay(SAME, -e, fore)),
            (1 + AG_LAG, relay(OTHER, 0, fore)),
            (2, relay(SAME, 2 * e, back, YY)),
            (2, relay(SAME, -2 * e, fore)),
            (2 + AG_LAG, relay(OTHER, -e, fore)),
            (3, relay(SAME, 3 * e, back, YY)),
            (3 + AG_LAG, relay(OTHER, -2 * e, fore)),
            (4, relay(SAME, 4, YY)),
            (5, finish),
        ]

    def weight_ready(i):
        local[i].wait()
        far[i].wait_recv()

    def project_kv(j):
        if j == 0:
            weight_ready(0)
        term = lax.dot_general(
            wkv[:, j * KC : (j + 1) * KC], xg[j], (((1,), (1,)), ((), ())),
            preferred_element_type=F32,
        )
        acckv[...] = term if j == 0 else acckv[...] + term

    def project_q(j):
        weight_ready(1 + j)
        for cc in range(2):
            term = jnp.dot(
                xg[j], wq[cc, j * KC : (j + 1) * KC, :], preferred_element_type=F32
            )
            span = slice(cc * 256, (cc + 1) * 256)
            accq[:, span] = term if j == 0 else accq[:, span] + term

    carry = pltpu.make_async_remote_copy(
        src_ref=carr, dst_ref=next_resid,
        send_sem=sh_s, recv_sem=sh_r,
        device_id=heirs[0], device_id_type=MESH,
    )

    def send_carry():
        carr[...] = (resid[...].astype(F32) + pending[...].astype(F32)).astype(BF16)
        carry.start()

    def send_weights():
        for copy in far:
            copy.start()

    def project(j):
        return lambda: project_kv(j)

    actions = [(0, send_weights)]
    if CARRY < 5:
        actions.append((CARRY, send_carry))
    for j in range(NC):
        actions += [(j * AG_LAP + when, act) for when, act in ag_actions(j)]
        if j < NC - 1:
            actions.append((j * AG_LAP + 5 + AG_MM, project(j)))
    for _, act in sorted(actions, key=lambda item: item[0]):
        act()

    project_kv(NC - 1)
    kvs[...] = acckv[...].astype(BF16)
    kv_rows = pl.ds(pl.multiple_of((z // 4) * 128 + yh * 64, 64), 64)
    kv_copies = []
    for yy in range(2):
        zz = 2 * (z % 4) + z // 4
        mine = (zz == z) & (yy == yh)
        copy = pltpu.make_async_remote_copy(
            src_ref=kvs, dst_ref=kvr.at[c, kv_rows],
            send_sem=kv_s.at[yy], recv_sem=kv_r.at[yh],
            device_id=at(zz, yy, c), device_id_type=MESH,
        )
        kv_copies.append((mine, copy))

        @pl.when(mine)
        def _():
            pltpu.make_async_copy(kvs, kvr.at[c, kv_rows], kv_r.at[yh]).start()

        @pl.when(jnp.logical_not(mine))
        def _(copy=copy):
            copy.start()

    if CARRY == 5.1:
        send_carry()
    for j in range(NC - 1):
        project_q(j)

    docs = doc_ids[...].astype(F32)
    row = lax.broadcasted_iota(jnp.int32, (TOK, 1), 0)
    mine_at = ((row // 16) * 32 + c * 16 + row % 16).astype(F32)
    key = lax.broadcasted_iota(jnp.int32, (1, 2 * TOK), 1)
    key_at = (((key % TOK) // 16) * 32 + (key // TOK) * 16 + key % 16).astype(F32)
    first = jnp.zeros((TOK, 1), F32)
    for k in range(1, 4):
        begin = jnp.sum(jnp.where(docs < k, 1.0, 0.0), axis=-1, keepdims=True)
        first = jnp.maximum(first, jnp.where(mine_at >= begin, begin, 0.0))
    mask = (key_at <= mine_at) & (key_at >= first)

    twin = at(z + 1 - 2 * (z % 2), yh, c)

    def kv_relay(i, kind, half, targets):
        rows = pl.ds(pl.multiple_of(kind * 128 + half * 64, 64), 64)
        ref = kvr.at[c, rows]
        pltpu.make_async_remote_copy(
            src_ref=ref, dst_ref=ref, send_sem=kv_s.at[0], recv_sem=kv_r.at[i],
            device_id=sibling, device_id_type=MESH,
        ).wait_recv()
        for n, (dev, slot) in enumerate(targets):
            copy = pltpu.make_async_remote_copy(
                src_ref=ref, dst_ref=ref,
                send_sem=kv_s.at[2 + 2 * i + n], recv_sem=kv_r.at[slot],
                device_id=dev, device_id_type=MESH,
            )
            copy.start()
            sends.append(copy)

    for half in range(2):
        kv_relay(half, z % 2, half, [(twin, 2 + half), (sibling, 4 + half)])
    if CARRY == 5.12:
        send_carry()
    project_q(NC - 1)
    for half in range(2):
        kv_relay(2 + half, 1 - z % 2, half, [(sibling, 6 + half)])
    if CARRY == 5.15:
        send_carry()
    for i in range(4):
        kind = z % 2 if i < 2 else 1 - z % 2
        rows = pl.ds(pl.multiple_of(kind * 128 + (i % 2) * 64, 64), 64)
        ref = kvr.at[1 - c, rows]
        pltpu.make_async_remote_copy(
            src_ref=ref, dst_ref=ref, send_sem=kv_s.at[0], recv_sem=kv_r.at[4 + i],
            device_id=sibling, device_id_type=MESH,
        ).wait_recv()

    if CARRY == 5.2:
        send_carry()
    keys = jnp.concatenate([kvr[0, :128, :], kvr[1, :128, :]], axis=1)
    values = jnp.concatenate([kvr[0, 128:, :], kvr[1, 128:, :]], axis=1)
    for h in range(4):
        query = accq[:, h * HD : (h + 1) * HD].astype(BF16)
        scores = jnp.dot(query, keys, preferred_element_type=F32) / math.sqrt(HD)
        scores = jnp.where(mask, scores, -1e30)
        top = jnp.max(scores, axis=-1, keepdims=True)
        weight = jnp.exp(scores - top)
        probs = (weight / jnp.sum(weight, axis=-1, keepdims=True)).astype(BF16)
        ctx[:, h * HD : (h + 1) * HD] = lax.dot_general(
            probs, values, (((1,), (1,)), ((), ())), preferred_element_type=F32
        ).astype(BF16)

    sent = [0] * NC

    def rs_send(j, kind, d, way, slot):
        copy = pltpu.make_async_remote_copy(
            src_ref=part.at[j, block(kind, d)], dst_ref=rsb.at[j, slot],
            send_sem=rs_s.at[j * 20 + sent[j]], recv_sem=rs_r.at[j * SLOTS + slot],
            device_id=neighbour[way], device_id_type=MESH,
        )
        sent[j] += 1
        copy.start()
        sends.append(copy)

    def rs_add(j, kind, d, slots):
        for slot in slots:
            ref = rsb.at[j, slot]
            pltpu.make_async_remote_copy(
                src_ref=ref, dst_ref=ref,
                send_sem=rs_s.at[j * 20], recv_sem=rs_r.at[j * SLOTS + slot],
                device_id=neighbour[YY], device_id_type=MESH,
            ).wait_recv()
        total = part[j, block(kind, d)].astype(F32)
        for slot in slots:
            total = total + rsb[j, slot].astype(F32)
        part[j, block(kind, d)] = total.astype(BF16)

    def hand_on(j, which):
        copy = pltpu.make_async_remote_copy(
            src_ref=part.at[j, block(which, 0)], dst_ref=fin.at[which, :, cols(j)],
            send_sem=fin_s.at[2 * j + which], recv_sem=fin_r.at[2 * j + which],
            device_id=heirs[which], device_id_type=MESH,
        )
        copy.start()
        handed.append(copy)

    handed = []

    def rs_actions(j):
        e = 1 if j % 2 == 0 else -1
        fore, back = (ZP, ZM) if e == 1 else (ZM, ZP)

        def begin():
            weight_ready(1 + NC + j)
            for n in range(0, KC, 512):
                part[j, :, n : n + 512] = jnp.dot(
                    ctx[...], wo[:, j * KC + n : j * KC + n + 512], preferred_element_type=F32
                ).astype(BF16)
            rs_send(j, OTHER, 4, YY, YE[4])
            rs_send(j, OTHER, -3 * e, back, QB[2])
            rs_send(j, SAME, -3 * e, back, RB[2])

        def cross(d):
            return lambda: rs_send(j, OTHER, d * e, YY, YE[d])

        def relay(kind, d, slots, way, slot):
            def act():
                rs_add(j, kind, d, slots)
                rs_send(j, kind, d, way, slot)

            return act

        def finish(kind, slots):
            def act():
                rs_add(j, kind, 0, slots)
                hand_on(j, kind)

            return act

        return [
            (0, begin),
            (RS_Y[0], cross(3)),
            (RS_Y[1], cross(2)),
            (RS_Y[2], cross(1)),
            (1, relay(SAME, 4, [YE[4]], fore, RF[3])),
            (1, relay(OTHER, -2 * e, [QB[2]], back, QB[1])),
            (1, relay(SAME, -2 * e, [RB[2]], back, RB[1])),
            (2, relay(SAME, 3 * e, [YE[3], RF[3]], fore, RF[2])),
            (2, relay(OTHER, -e, [QB[1]], back, QB[0])),
            (2, relay(SAME, -e, [RB[1]], back, RB[0])),
            (3, relay(SAME, 2 * e, [YE[2], RF[2]], fore, RF[1])),
            (3, finish(OTHER, [QB[0]])),
            (4, relay(SAME, e, [YE[1], RF[1]], fore, RF[0])),
            (5, finish(SAME, [RF[0], RB[0]])),
        ]

    actions = []
    if CARRY >= 6:
        actions.append((CARRY - 6, send_carry))
    for j in range(NC):
        actions += [(j * RS_LAP + when, act) for when, act in rs_actions(j)]
    for _, act in sorted(actions, key=lambda item: item[0]):
        act()

    for j in range(NC):
        for which in range(2):
            ref = fin.at[which, :, cols(j)]
            pltpu.make_async_remote_copy(
                src_ref=ref, dst_ref=ref,
                send_sem=fin_s.at[0], recv_sem=fin_r.at[2 * j + which],
                device_id=heirs[0], device_id_type=MESH,
            ).wait_recv()

    for copy in sends:
        copy.wait_send()
    for copy in far:
        copy.wait_send()
    for mine, copy in kv_copies:

        @pl.when(jnp.logical_not(mine))
        def _(copy=copy):
            copy.wait_send()

    carry.wait()
    for copy in handed:
        copy.wait_send()


def finish_kernel(carried, sums, next_resid, next_output):
    next_resid[...] = carried[...]
    next_output[...] = (sums[0].astype(F32) + sums[1].astype(F32)).astype(BF16)


def body(resid, pending, doc_ids, norm_gain, q_weight, kv_weight, o_weight):
    vmem = pl.BlockSpec(memory_space=pltpu.VMEM)
    hbm = pl.BlockSpec(memory_space=pltpu.HBM)
    dma = pltpu.SemaphoreType.DMA
    carried, sums = pl.pallas_call(
        kernel,
        out_shape=(
            jax.ShapeDtypeStruct((ROWS, D), BF16),
            jax.ShapeDtypeStruct((2, ROWS, D), BF16),
        ),
        in_specs=[vmem] * 4 + [hbm] * 3,
        out_specs=(hbm, hbm),
        scratch_shapes=[
            pltpu.VMEM((NC, TOK, KC), BF16),
            pltpu.VMEM((2, D, 256), BF16),
            pltpu.VMEM((64, D), BF16),
            pltpu.VMEM((512, D), BF16),
            pltpu.VMEM((TOK, 512), F32),
            pltpu.VMEM((64, TOK), F32),
            pltpu.VMEM((64, TOK), BF16),
            pltpu.VMEM((2, 256, TOK), BF16),
            pltpu.VMEM((TOK, 512), BF16),
            pltpu.VMEM((NC, TOK, KC), BF16),
            pltpu.VMEM((NC, SLOTS, ROWS, KC), BF16),
            pltpu.VMEM((ROWS, D), BF16),
            dma((NC * 16,)),
            dma((NC * 16,)),
            dma((NC * 20,)),
            dma((NC * SLOTS,)),
            dma((10,)),
            dma((8,)),
            dma((1 + 2 * NC,)),
            dma((1 + 2 * NC,)),
            dma((1 + 2 * NC,)),
            dma,
            dma,
            dma((2 * NC,)),
            dma((2 * NC,)),
        ],
        compiler_params=pltpu.CompilerParams(
            collective_id=0, has_side_effects=True, vmem_limit_bytes=VMEM << 20
        ),
        name="module",
    )(
        resid[0], pending[0], doc_ids, norm_gain,
        q_weight[0], kv_weight[0].T, o_weight[0],
    )
    if FINISH == 0:
        return carried[None], (sums[0].astype(F32) + sums[1].astype(F32)).astype(BF16)[None]
    out = jax.ShapeDtypeStruct((ROWS, D), BF16)
    next_resid, next_output = pl.pallas_call(
        finish_kernel,
        out_shape=(out, out),
        in_specs=[vmem, vmem],
        out_specs=(vmem, vmem),
        compiler_params=pltpu.CompilerParams(vmem_limit_bytes=VMEM << 20),
        name="finish",
    )(carried, sums)
    return next_resid[None], next_output[None]


def solution(mesh):
    in_specs = (
        P("section", "tp", None),
        P("section", "tp", None),
        P("section", None),
        P("section", None),
        P("section", None, "tp"),
        P("section", None, "tp"),
        P("section", "tp", None),
    )
    out_specs = (P("section", "tp", None), P("section", "tp", None))
    return jax.shard_map(body, mesh=mesh, in_specs=in_specs, out_specs=out_specs, check_vma=False)
```

```python
import functools
import jax
import jax.numpy as jnp
from jax import lax
from jax.experimental import pallas as pl
from jax.experimental.pallas import tpu as pltpu
from jax.sharding import PartitionSpec as P

D = 8192
HD = 128
Z = 8
ROWS = 16
TOK = 256
NC = 4
KC = D // NC
VMEM = 56
FINISH = 1
AG_LAP = 0.25
AG_LAG = 1.1
KV_ORDER = (0, 1, 2, 3)
T_F = (1, 2, 3, 4)
T_Q = (1, 2)
T_B = (0, 1.5, 2.5)
AG_MM = 0.5
RS_LAP = 0
RS_Q = 3
RS_Y = (0.1, 0.2, 0.3)
CARRY = 5.12
MESH = pl.DeviceIdType.MESH
F32 = jnp.float32
BF16 = jnp.bfloat16
SAME, OTHER = 0, 1
ZP, ZM, YY = 0, 1, 2

YE = {4: 0, 3: 1, 2: 2, 1: 3}
RF = {3: 4, 2: 5, 1: 6, 0: 7}
RB = {2: 8, 1: 9, 0: 10}
QB = {2: 11, 1: 12, 0: 13}
SLOTS = 14


def kernel(
    resid, pending, doc_ids, gain, wq_hbm, wkv_hbm, wo_hbm,
    next_resid, fin,
    xg, wq, wkv, wo, accq, acckv, kvs, kvr, ctx, part, rsb, carr,
    ag_s, ag_r, rs_s, rs_r, kv_s, kv_r, lw, ws, wr, sh_s, sh_r, fin_s, fin_r,
):
    sec = lax.axis_index("section")
    t = lax.axis_index("tp")
    z, yh, c = t // 4, (t // 2) % 2, t % 2

    def at(zz, yy, cc):
        return (sec, (zz * 2 + yy) * 2 + cc)

    neighbour = (
        at((z + 1) % Z, yh, c),
        at((z + Z - 1) % Z, yh, c),
        at(z, 1 - yh, c),
    )
    sibling = at(z, yh, 1 - c)
    across = (z * 2 + 1 - yh) * 2 + c
    after, before = (sec + 1) % 8, (sec + 7) % 8
    heirs = ((after, t), (after, across))

    def block(kind, d):
        b = ((z + d + Z) % Z) * 2 + (yh if kind == SAME else 1 - yh)
        return pl.ds(pl.multiple_of(b * ROWS, ROWS), ROWS)

    barrier = pltpu.get_barrier_semaphore()
    for o in range(1, 32):
        pl.semaphore_signal(barrier, inc=1, device_id=(sec, (t + o) % 32), device_id_type=MESH)
    for dev in (*heirs, (before, t), (before, across)):
        pl.semaphore_signal(barrier, inc=1, device_id=dev, device_id_type=MESH)

    def cols(j):
        return pl.ds(j * KC, KC)

    pieces = [(wkv_hbm, wkv.at[pl.ds(pl.multiple_of(c * 32, 32), 32)])]
    for j in range(NC):
        pieces.append((wq_hbm.at[cols(j)], wq.at[c, cols(j)]))
    for j in range(NC):
        pieces.append(
            (wo_hbm.at[:, cols(j)], wo.at[pl.ds(pl.multiple_of(c * 256, 256), 256), cols(j)])
        )
    local = [pltpu.make_async_copy(s, d, lw.at[i]) for i, (s, d) in enumerate(pieces)]
    far = [
        pltpu.make_async_remote_copy(
            src_ref=s, dst_ref=d, send_sem=ws.at[i], recv_sem=wr.at[i],
            device_id=sibling, device_id_type=MESH,
        )
        for i, (s, d) in enumerate(pieces)
    ]
    for copy in local:
        copy.start()

    stream = resid[...].astype(F32)
    scale = lax.rsqrt(jnp.mean(stream * stream, axis=-1, keepdims=True) + 1e-05)
    pl.semaphore_wait(barrier, 35)

    sends = []

    count = [0] * NC

    def ag_send(j, kind, d, way):
        dd = d - 1 if way == ZP else d + 1 if way == ZM else d
        kk = kind if way != YY else 1 - kind
        ref = xg.at[j, block(kind, d)]
        copy = pltpu.make_async_remote_copy(
            src_ref=ref, dst_ref=ref,
            send_sem=ag_s.at[j * 16 + count[j]], recv_sem=ag_r.at[j * 16 + kk * 8 + dd % 8],
            device_id=neighbour[way], device_id_type=MESH,
        )
        count[j] += 1
        copy.start()
        sends.append(copy)

    def ag_wait(j, kind, d):
        ref = xg.at[j, block(kind, d)]
        pltpu.make_async_remote_copy(
            src_ref=ref, dst_ref=ref,
            send_sem=ag_s.at[j * 16], recv_sem=ag_r.at[j * 16 + kind * 8 + d % 8],
            device_id=neighbour[YY], device_id_type=MESH,
        ).wait_recv()

    def ag_actions(j):
        e = 1 if j % 2 == 0 else -1
        fore, back = (ZP, ZM) if e == 1 else (ZM, ZP)

        def begin():
            piece = resid[:, j * KC : (j + 1) * KC].astype(F32)
            xg[j, block(SAME, 0)] = (
                piece * scale * gain[:, j * KC : (j + 1) * KC].astype(F32)
            ).astype(BF16)
            for way in (back, fore, YY):
                ag_send(j, SAME, 0, way)

        def relay(kind, d, *ways):
            def act():
                ag_wait(j, kind, d)
                for way in ways:
                    ag_send(j, kind, d, way)

            return act

        def finish():
            for kind, d in ((SAME, -3), (OTHER, 1), (OTHER, 2), (OTHER, 3), (OTHER, -3), (OTHER, 4)):
                ag_wait(j, kind, d * e if d != 4 else 4)

        return [
            (0, begin),
            (1, relay(SAME, e, back, YY)),
            (1, relay(SAME, -e, fore)),
            (1 + AG_LAG, relay(OTHER, 0, fore)),
            (2, relay(SAME, 2 * e, back, YY)),
            (2, relay(SAME, -2 * e, fore)),
            (2 + AG_LAG, relay(OTHER, -e, fore)),
            (3, relay(SAME, 3 * e, back, YY)),
            (3 + AG_LAG, relay(OTHER, -2 * e, fore)),
            (4, relay(SAME, 4, YY)),
            (5, finish),
        ]

    def weight_ready(i):
        local[i].wait()
        far[i].wait_recv()

    def project_kv(j):
        if j == 0:
            weight_ready(0)
        term = lax.dot_general(
            wkv[:, j * KC : (j + 1) * KC], xg[j], (((1,), (1,)), ((), ())),
            preferred_element_type=F32,
        )
        acckv[...] = term if j == 0 else acckv[...] + term

    def project_q(j):
        weight_ready(1 + j)
        for cc in range(2):
            term = jnp.dot(
                xg[j], wq[cc, j * KC : (j + 1) * KC, :], preferred_element_type=F32
            )
            span = slice(cc * 256, (cc + 1) * 256)
            accq[:, span] = term if j == 0 else accq[:, span] + term

    carry = pltpu.make_async_remote_copy(
        src_ref=carr, dst_ref=next_resid,
        send_sem=sh_s, recv_sem=sh_r,
        device_id=heirs[0], device_id_type=MESH,
    )

    def send_carry():
        carr[...] = (resid[...].astype(F32) + pending[...].astype(F32)).astype(BF16)
        carry.start()

    def send_weights():
        for copy in far:
            copy.start()

    def project(j):
        return lambda: project_kv(j)

    actions = [(0, send_weights)]
    if CARRY < 5:
        actions.append((CARRY, send_carry))
    for j in range(NC):
        actions += [(j * AG_LAP + when, act) for when, act in ag_actions(j)]
        if j < NC - 1:
            actions.append((j * AG_LAP + 5 + AG_MM, project(j)))
    for _, act in sorted(actions, key=lambda item: item[0]):
        act()

    project_kv(NC - 1)
    kvs[...] = acckv[...].astype(BF16)
    kv_rows = pl.ds(pl.multiple_of((z // 4) * 128 + yh * 64, 64), 64)
    kv_copies = []
    for n in range(4):
        zz, yy = 2 * (z % 4) + n // 2, n % 2
        mine = (zz == z) & (yy == yh)
        copy = pltpu.make_async_remote_copy(
            src_ref=kvs, dst_ref=kvr.at[c, kv_rows],
            send_sem=kv_s.at[n], recv_sem=kv_r.at[z // 4 * 2 + yh],
            device_id=at(zz, yy, c), device_id_type=MESH,
        )
        kv_copies.append((mine, copy))

        @pl.when(mine)
        def _():
            pltpu.make_async_copy(kvs, kvr.at[c, kv_rows], kv_r.at[z // 4 * 2 + yh]).start()

        @pl.when(jnp.logical_not(mine))
        def _(copy=copy):
            copy.start()

    if CARRY == 5.1:
        send_carry()
    for j in range(NC - 1):
        project_q(j)

    docs = doc_ids[...].astype(F32)
    row = lax.broadcasted_iota(jnp.int32, (TOK, 1), 0)
    mine_at = ((row // 16) * 32 + c * 16 + row % 16).astype(F32)
    key = lax.broadcasted_iota(jnp.int32, (1, 2 * TOK), 1)
    key_at = (((key % TOK) // 16) * 32 + (key // TOK) * 16 + key % 16).astype(F32)
    first = jnp.zeros((TOK, 1), F32)
    for k in range(1, 4):
        begin = jnp.sum(jnp.where(docs < k, 1.0, 0.0), axis=-1, keepdims=True)
        first = jnp.maximum(first, jnp.where(mine_at >= begin, begin, 0.0))
    mask = (key_at <= mine_at) & (key_at >= first)


    def kv_relay(i, kind, half, targets):
        rows = pl.ds(kind * 128 + half * 64, 64)
        ref = kvr.at[c, rows]
        pltpu.make_async_remote_copy(
            src_ref=ref, dst_ref=ref, send_sem=kv_s.at[0], recv_sem=kv_r.at[i],
            device_id=sibling, device_id_type=MESH,
        ).wait_recv()
        for dev, slot in targets:
            copy = pltpu.make_async_remote_copy(
                src_ref=ref, dst_ref=ref,
                send_sem=kv_s.at[4 + i], recv_sem=kv_r.at[slot],
                device_id=dev, device_id_type=MESH,
            )
            copy.start()
            sends.append(copy)

    if CARRY == 5.12:
        send_carry()
    project_q(NC - 1)
    for i in KV_ORDER:
        kv_relay(i, i // 2, i % 2, [(sibling, 4 + i)])
    if CARRY == 5.15:
        send_carry()
    for i in range(4):
        rows = pl.ds(i * 64, 64)
        ref = kvr.at[1 - c, rows]
        pltpu.make_async_remote_copy(
            src_ref=ref, dst_ref=ref, send_sem=kv_s.at[0], recv_sem=kv_r.at[4 + i],
            device_id=sibling, device_id_type=MESH,
        ).wait_recv()

    if CARRY == 5.2:
        send_carry()
    keys = jnp.concatenate([kvr[0, :128, :], kvr[1, :128, :]], axis=1)
    values = jnp.concatenate([kvr[0, 128:, :], kvr[1, 128:, :]], axis=1)
    for h in range(4):
        query = accq[:, h * HD : (h + 1) * HD].astype(BF16)
        scores = jnp.dot(query, keys, preferred_element_type=F32) * HD**-0.5
        scores = jnp.where(mask, scores, -1e30)
        top = jnp.max(scores, axis=-1, keepdims=True)
        weight = jnp.exp(scores - top)
        probs = (weight * (1.0 / jnp.sum(weight, axis=-1, keepdims=True))).astype(BF16)
        ctx[:, h * HD : (h + 1) * HD] = lax.dot_general(
            probs, values, (((1,), (1,)), ((), ())), preferred_element_type=F32
        ).astype(BF16)

    sent = [0] * NC

    def rs_send(j, kind, d, way, slot):
        copy = pltpu.make_async_remote_copy(
            src_ref=part.at[j, block(kind, d)], dst_ref=rsb.at[j, slot],
            send_sem=rs_s.at[j * 20 + sent[j]], recv_sem=rs_r.at[j * SLOTS + slot],
            device_id=neighbour[way], device_id_type=MESH,
        )
        sent[j] += 1
        copy.start()
        sends.append(copy)

    def rs_add(j, kind, d, slots):
        for slot in slots:
            ref = rsb.at[j, slot]
            pltpu.make_async_remote_copy(
                src_ref=ref, dst_ref=ref,
                send_sem=rs_s.at[j * 20], recv_sem=rs_r.at[j * SLOTS + slot],
                device_id=neighbour[YY], device_id_type=MESH,
            ).wait_recv()
        total = part[j, block(kind, d)].astype(F32)
        for slot in slots:
            total = total + rsb[j, slot].astype(F32)
        part[j, block(kind, d)] = total.astype(BF16)

    def hand_on(j, which):
        copy = pltpu.make_async_remote_copy(
            src_ref=part.at[j, block(which, 0)], dst_ref=fin.at[which, :, cols(j)],
            send_sem=fin_s.at[2 * j + which], recv_sem=fin_r.at[2 * j + which],
            device_id=heirs[which], device_id_type=MESH,
        )
        copy.start()
        handed.append(copy)

    handed = []

    def rs_actions(j):
        e = 1 if j % 2 == 0 else -1
        fore, back = (ZP, ZM) if e == 1 else (ZM, ZP)

        def begin():
            weight_ready(1 + NC + j)
            for n in range(0, KC, 512):
                part[j, :, n : n + 512] = jnp.dot(
                    ctx[...], wo[:, j * KC + n : j * KC + n + 512], preferred_element_type=F32
                ).astype(BF16)
            rs_send(j, OTHER, 4, YY, YE[4])
            rs_send(j, OTHER, -3 * e, back, QB[2])

        def cross(d):
            return lambda: rs_send(j, OTHER, d * e, YY, YE[d])

        def relay(kind, d, slots, way, slot):
            def act():
                rs_add(j, kind, d, slots)
                rs_send(j, kind, d, way, slot)

            return act

        def finish(kind, slots):
            def act():
                rs_add(j, kind, 0, slots)
                hand_on(j, kind)

            return act

        return [
            (0, begin),
            (RS_Y[0], cross(3)),
            (RS_Y[1], cross(2)),
            (RS_Y[2], cross(1)),
            (T_B[0], lambda: rs_send(j, SAME, -3 * e, back, RB[2])),
            (T_F[0], relay(SAME, 4, [YE[4]], fore, RF[3])),
            (T_Q[0], relay(OTHER, -2 * e, [QB[2]], back, QB[1])),
            (T_B[1], relay(SAME, -2 * e, [RB[2]], back, RB[1])),
            (T_F[1], relay(SAME, 3 * e, [YE[3], RF[3]], fore, RF[2])),
            (T_Q[1], relay(OTHER, -e, [QB[1]], back, QB[0])),
            (T_B[2], relay(SAME, -e, [RB[1]], back, RB[0])),
            (T_F[2], relay(SAME, 2 * e, [YE[2], RF[2]], fore, RF[1])),
            (RS_Q, finish(OTHER, [QB[0]])),
            (T_F[3], relay(SAME, e, [YE[1], RF[1]], fore, RF[0])),
            (5, finish(SAME, [RF[0], RB[0]])),
        ]

    actions = []
    if CARRY >= 6:
        actions.append((CARRY - 6, send_carry))
    for j in range(NC):
        actions += [(j * RS_LAP + when, act) for when, act in rs_actions(j)]
    for _, act in sorted(actions, key=lambda item: item[0]):
        act()

    for j in range(NC):
        for which in range(2):
            ref = fin.at[which, :, cols(j)]
            pltpu.make_async_remote_copy(
                src_ref=ref, dst_ref=ref,
                send_sem=fin_s.at[0], recv_sem=fin_r.at[2 * j + which],
                device_id=heirs[0], device_id_type=MESH,
            ).wait_recv()

    for copy in sends:
        copy.wait_send()
    for copy in far:
        copy.wait_send()
    for mine, copy in kv_copies:

        @pl.when(jnp.logical_not(mine))
        def _(copy=copy):
            copy.wait_send()

    carry.wait()
    for copy in handed:
        copy.wait_send()


def finish_kernel(carried, sums, next_resid, next_output):
    next_resid[...] = carried[...]
    next_output[...] = (sums[0].astype(F32) + sums[1].astype(F32)).astype(BF16)


def body(resid, pending, doc_ids, norm_gain, q_weight, kv_weight, o_weight):
    vmem = pl.BlockSpec(memory_space=pltpu.VMEM)
    hbm = pl.BlockSpec(memory_space=pltpu.HBM)
    dma = pltpu.SemaphoreType.DMA
    carried, sums = pl.pallas_call(
        kernel,
        out_shape=(
            jax.ShapeDtypeStruct((ROWS, D), BF16),
            jax.ShapeDtypeStruct((2, ROWS, D), BF16),
        ),
        in_specs=[vmem] * 4 + [hbm] * 3,
        out_specs=(hbm, hbm),
        scratch_shapes=[
            pltpu.VMEM((NC, TOK, KC), BF16),
            pltpu.VMEM((2, D, 256), BF16),
            pltpu.VMEM((64, D), BF16),
            pltpu.VMEM((512, D), BF16),
            pltpu.VMEM((TOK, 512), F32),
            pltpu.VMEM((64, TOK), F32),
            pltpu.VMEM((64, TOK), BF16),
            pltpu.VMEM((2, 256, TOK), BF16),
            pltpu.VMEM((TOK, 512), BF16),
            pltpu.VMEM((NC, TOK, KC), BF16),
            pltpu.VMEM((NC, SLOTS, ROWS, KC), BF16),
            pltpu.VMEM((ROWS, D), BF16),
            dma((NC * 16,)),
            dma((NC * 16,)),
            dma((NC * 20,)),
            dma((NC * SLOTS,)),
            dma((10,)),
            dma((8,)),
            dma((1 + 2 * NC,)),
            dma((1 + 2 * NC,)),
            dma((1 + 2 * NC,)),
            dma,
            dma,
            dma((2 * NC,)),
            dma((2 * NC,)),
        ],
        compiler_params=pltpu.CompilerParams(
            collective_id=0, has_side_effects=True, vmem_limit_bytes=VMEM << 20
        ),
        name="module",
    )(
        resid[0], pending[0], doc_ids, norm_gain,
        q_weight[0], kv_weight[0].T, o_weight[0],
    )
    if FINISH == 0:
        return carried[None], (sums[0].astype(F32) + sums[1].astype(F32)).astype(BF16)[None]
    out = jax.ShapeDtypeStruct((ROWS, D), BF16)
    next_resid, next_output = pl.pallas_call(
        finish_kernel,
        out_shape=(out, out),
        in_specs=[vmem, vmem],
        out_specs=(vmem, vmem),
        compiler_params=pltpu.CompilerParams(vmem_limit_bytes=VMEM << 20),
        name="finish",
    )(carried, sums)
    return next_resid[None], next_output[None]


def solution(mesh):
    in_specs = (
        P("section", "tp", None),
        P("section", "tp", None),
        P("section", None),
        P("section", None),
        P("section", None, "tp"),
        P("section", None, "tp"),
        P("section", "tp", None),
    )
    out_specs = (P("section", "tp", None), P("section", "tp", None))
    return jax.shard_map(body, mesh=mesh, in_specs=in_specs, out_specs=out_specs, check_vma=False)
```

```python
import functools
import jax
import jax.numpy as jnp
from jax import lax
from jax.experimental import pallas as pl
from jax.experimental.pallas import tpu as pltpu
from jax.sharding import PartitionSpec as P

D = 8192
HD = 128
Z = 8
ROWS = 16
TOK = 256
NC = 4
KC = D // NC
VMEM = 56
AG_LAP = 0.25
AG_LAG = 1.1
KV_ORDER = (0, 1, 2, 3)
T_F = (1, 2, 3, 4)
T_Q = (1, 2)
T_B = (0, 1.5, 2.5)
AG_MM = 0.5
RS_LAP = 0
RS_Q = 2.5
RS_Y = (0.1, 0.2, 0.3)
MESH = pl.DeviceIdType.MESH
F32 = jnp.float32
BF16 = jnp.bfloat16
SAME, OTHER = 0, 1
ZP, ZM, YY = 0, 1, 2

YE = {4: 0, 3: 1, 2: 2, 1: 3}
RF = {3: 4, 2: 5, 1: 6, 0: 7}
RB = {2: 8, 1: 9, 0: 10}
QB = {2: 11, 1: 12, 0: 13}
SLOTS = 14


def kernel(
    resid, pending, doc_ids, gain, wq_hbm, wkv_hbm, wo_hbm,
    next_resid, fin,
    xg, wq, wkv, wo, accq, acckv, kvs, kvr, ctx, part, rsb, carr,
    ag_s, ag_r, rs_s, rs_r, kv_s, kv_r, lw, ws, wr, sh_s, sh_r, fin_s, fin_r,
):
    sec = lax.axis_index("section")
    t = lax.axis_index("tp")
    z, yh, c = t // 4, (t // 2) % 2, t % 2

    def at(zz, yy, cc):
        return (sec, (zz * 2 + yy) * 2 + cc)

    neighbour = (
        at((z + 1) % Z, yh, c),
        at((z + Z - 1) % Z, yh, c),
        at(z, 1 - yh, c),
    )
    sibling = at(z, yh, 1 - c)
    across = (z * 2 + 1 - yh) * 2 + c
    after, before = (sec + 1) % 8, (sec + 7) % 8
    heirs = ((after, t), (after, across))

    def block(kind, d):
        b = ((z + d + Z) % Z) * 2 + (yh if kind == SAME else 1 - yh)
        return pl.ds(pl.multiple_of(b * ROWS, ROWS), ROWS)

    barrier = pltpu.get_barrier_semaphore()
    for o in range(2, 32, 2):
        pl.semaphore_signal(barrier, inc=1, device_id=(sec, (t + o) % 32), device_id_type=MESH)
    for dev in (sibling, *heirs, (before, t), (before, across)):
        pl.semaphore_signal(barrier, inc=1, device_id=dev, device_id_type=MESH)

    def cols(j):
        return pl.ds(j * KC, KC)

    pieces = [(wkv_hbm, wkv.at[pl.ds(pl.multiple_of(c * 32, 32), 32)])]
    for j in range(NC):
        pieces.append((wq_hbm.at[cols(j)], wq.at[c, cols(j)]))
    for j in range(NC):
        pieces.append(
            (wo_hbm.at[:, cols(j)], wo.at[pl.ds(pl.multiple_of(c * 256, 256), 256), cols(j)])
        )
    local = [pltpu.make_async_copy(s, d, lw.at[i]) for i, (s, d) in enumerate(pieces)]
    far = [
        pltpu.make_async_remote_copy(
            src_ref=s, dst_ref=d, send_sem=ws.at[i], recv_sem=wr.at[i],
            device_id=sibling, device_id_type=MESH,
        )
        for i, (s, d) in enumerate(pieces)
    ]
    for copy in local:
        copy.start()

    stream = resid[...].astype(F32)
    scale = lax.rsqrt(jnp.mean(stream * stream, axis=-1, keepdims=True) + 1e-05)
    pl.semaphore_wait(barrier, 20)

    sends = []

    count = [0] * NC

    def ag_send(j, kind, d, way):
        dd = d - 1 if way == ZP else d + 1 if way == ZM else d
        kk = kind if way != YY else 1 - kind
        ref = xg.at[j, block(kind, d)]
        copy = pltpu.make_async_remote_copy(
            src_ref=ref, dst_ref=ref,
            send_sem=ag_s.at[j * 16 + count[j]], recv_sem=ag_r.at[j * 16 + kk * 8 + dd % 8],
            device_id=neighbour[way], device_id_type=MESH,
        )
        count[j] += 1
        copy.start()
        sends.append(copy)

    def ag_wait(j, kind, d):
        ref = xg.at[j, block(kind, d)]
        pltpu.make_async_remote_copy(
            src_ref=ref, dst_ref=ref,
            send_sem=ag_s.at[j * 16], recv_sem=ag_r.at[j * 16 + kind * 8 + d % 8],
            device_id=neighbour[YY], device_id_type=MESH,
        ).wait_recv()

    def ag_actions(j):
        e = 1 if j % 2 == 0 else -1
        fore, back = (ZP, ZM) if e == 1 else (ZM, ZP)

        def begin():
            piece = resid[:, j * KC : (j + 1) * KC].astype(F32)
            xg[j, block(SAME, 0)] = (
                piece * scale * gain[:, j * KC : (j + 1) * KC].astype(F32)
            ).astype(BF16)
            for way in (back, fore, YY):
                ag_send(j, SAME, 0, way)

        def relay(kind, d, *ways):
            def act():
                ag_wait(j, kind, d)
                for way in ways:
                    ag_send(j, kind, d, way)

            return act

        def finish():
            for kind, d in ((SAME, -3), (OTHER, 1), (OTHER, 2), (OTHER, 3), (OTHER, -3), (OTHER, 4)):
                ag_wait(j, kind, d * e if d != 4 else 4)

        return [
            (0, begin),
            (1, relay(SAME, e, back, YY)),
            (1, relay(SAME, -e, fore)),
            (1 + AG_LAG, relay(OTHER, 0, fore)),
            (2, relay(SAME, 2 * e, back, YY)),
            (2, relay(SAME, -2 * e, fore)),
            (2 + AG_LAG, relay(OTHER, -e, fore)),
            (3, relay(SAME, 3 * e, back, YY)),
            (3 + AG_LAG, relay(OTHER, -2 * e, fore)),
            (4, relay(SAME, 4, YY)),
            (5, finish),
        ]

    def weight_ready(i):
        local[i].wait()
        far[i].wait_recv()

    def project_kv(j):
        if j == 0:
            weight_ready(0)
        term = lax.dot_general(
            wkv[:, j * KC : (j + 1) * KC], xg[j], (((1,), (1,)), ((), ())),
            preferred_element_type=F32,
        )
        acckv[...] = term if j == 0 else acckv[...] + term

    def project_q(j):
        weight_ready(1 + j)
        for cc in range(2):
            term = jnp.dot(
                xg[j], wq[cc, j * KC : (j + 1) * KC, :], preferred_element_type=F32
            )
            span = slice(cc * 256, (cc + 1) * 256)
            accq[:, span] = term if j == 0 else accq[:, span] + term

    carry = pltpu.make_async_remote_copy(
        src_ref=carr, dst_ref=next_resid,
        send_sem=sh_s, recv_sem=sh_r,
        device_id=heirs[0], device_id_type=MESH,
    )

    def send_carry():
        carr[...] = (resid[...].astype(F32) + pending[...].astype(F32)).astype(BF16)
        carry.start()

    def send_weights():
        for copy in far:
            copy.start()

    def project(j):
        return lambda: project_kv(j)

    actions = [(0, send_weights)]
    for j in range(NC):
        actions += [(j * AG_LAP + when, act) for when, act in ag_actions(j)]
        if j < NC - 1:
            actions.append((j * AG_LAP + 5 + AG_MM, project(j)))
    for _, act in sorted(actions, key=lambda item: item[0]):
        act()

    project_kv(NC - 1)
    kvs[...] = acckv[...].astype(BF16)
    kv_rows = pl.ds(pl.multiple_of((z // 4) * 128 + yh * 64, 64), 64)
    kv_copies = []
    for n in range(4):
        zz, yy = 2 * (z % 4) + (n // 2 + 1 - z // 4) % 2, (n + 1 + yh) % 2
        mine = (zz == z) & (yy == yh)
        copy = pltpu.make_async_remote_copy(
            src_ref=kvs, dst_ref=kvr.at[c, kv_rows],
            send_sem=kv_s.at[n], recv_sem=kv_r.at[z // 4 * 2 + yh],
            device_id=at(zz, yy, c), device_id_type=MESH,
        )
        kv_copies.append((mine, copy))

        @pl.when(mine)
        def _():
            pltpu.make_async_copy(kvs, kvr.at[c, kv_rows], kv_r.at[z // 4 * 2 + yh]).start()

        @pl.when(jnp.logical_not(mine))
        def _(copy=copy):
            copy.start()

    for j in range(NC - 1):
        project_q(j)

    docs = doc_ids[...].astype(F32)
    key = lax.broadcasted_iota(jnp.int32, (1, 2 * TOK), 1)
    key_at = (((key % TOK) // 16) * 32 + (key // TOK) * 16 + key % 16).astype(F32)
    begins = [
        jnp.sum(jnp.where(docs < k, 1.0, 0.0), axis=-1, keepdims=True) for k in range(1, 4)
    ]

    def planes(g):
        return [
            pl.ds(pl.multiple_of((z + 2 + 4 * g + k) % Z * 32, 32), 32) for k in range(4)
        ]

    def mask_of(g):
        row = lax.broadcasted_iota(jnp.int32, (TOK // 2, 1), 0)
        plane = (z + 2 + 4 * g + row // 32) % Z
        mine_at = (plane * 64 + row % 32 // 16 * 32 + c * 16 + row % 16).astype(F32)
        first = jnp.zeros((TOK // 2, 1), F32)
        for begin in begins:
            first = jnp.maximum(first, jnp.where(mine_at >= begin, begin, 0.0))
        return (key_at <= mine_at) & (key_at >= first)

    mask = mask_of(0)

    def kv_relay(i, kind, half, targets):
        rows = pl.ds(kind * 128 + half * 64, 64)
        ref = kvr.at[c, rows]
        pltpu.make_async_remote_copy(
            src_ref=ref, dst_ref=ref, send_sem=kv_s.at[0], recv_sem=kv_r.at[i],
            device_id=sibling, device_id_type=MESH,
        ).wait_recv()
        for dev, slot in targets:
            copy = pltpu.make_async_remote_copy(
                src_ref=ref, dst_ref=ref,
                send_sem=kv_s.at[4 + i], recv_sem=kv_r.at[slot],
                device_id=dev, device_id_type=MESH,
            )
            copy.start()
            sends.append(copy)

    send_carry()
    project_q(NC - 1)
    for i in KV_ORDER:
        kv_relay(i, i // 2, i % 2, [(sibling, 4 + i)])
    for i in range(4):
        rows = pl.ds(i * 64, 64)
        ref = kvr.at[1 - c, rows]
        pltpu.make_async_remote_copy(
            src_ref=ref, dst_ref=ref, send_sem=kv_s.at[0], recv_sem=kv_r.at[4 + i],
            device_id=sibling, device_id_type=MESH,
        ).wait_recv()

    keys = jnp.concatenate([kvr[0, :128, :], kvr[1, :128, :]], axis=1)
    values = jnp.concatenate([kvr[0, 128:, :], kvr[1, 128:, :]], axis=1)
    def attend(g, mask):
        for h in range(4):
            span = slice(h * HD, (h + 1) * HD)
            query = jnp.concatenate([accq[rows, span] for rows in planes(g)], axis=0).astype(BF16)
            scores = jnp.dot(query, keys, preferred_element_type=F32) * HD**-0.5
            scores = jnp.where(mask, scores, -1e30)
            top = jnp.max(scores, axis=-1, keepdims=True)
            weight = jnp.exp(scores - top)
            probs = (weight * (1.0 / jnp.sum(weight, axis=-1, keepdims=True))).astype(BF16)
            ctx[g, :, span] = lax.dot_general(
                probs, values, (((1,), (1,)), ((), ())), preferred_element_type=F32
            ).astype(BF16)

    def out_project(j, g):
        for n in range(0, KC, 512):
            term = jnp.dot(
                ctx[g], wo[:, j * KC + n : j * KC + n + 512], preferred_element_type=F32
            ).astype(BF16)
            for k, rows in enumerate(planes(g)):
                part[j, rows, n : n + 512] = term[k * 32 : (k + 1) * 32]

    attend(0, mask)

    sent = [0] * NC

    def rs_send(j, kind, d, way, slot):
        copy = pltpu.make_async_remote_copy(
            src_ref=part.at[j, block(kind, d)], dst_ref=rsb.at[j, slot],
            send_sem=rs_s.at[j * 20 + sent[j]], recv_sem=rs_r.at[j * SLOTS + slot],
            device_id=neighbour[way], device_id_type=MESH,
        )
        sent[j] += 1
        copy.start()
        sends.append(copy)

    def rs_add(j, kind, d, slots):
        for slot in slots:
            ref = rsb.at[j, slot]
            pltpu.make_async_remote_copy(
                src_ref=ref, dst_ref=ref,
                send_sem=rs_s.at[j * 20], recv_sem=rs_r.at[j * SLOTS + slot],
                device_id=neighbour[YY], device_id_type=MESH,
            ).wait_recv()
        total = part[j, block(kind, d)].astype(F32)
        for slot in slots:
            total = total + rsb[j, slot].astype(F32)
        part[j, block(kind, d)] = total.astype(BF16)

    def hand_on(j, which):
        copy = pltpu.make_async_remote_copy(
            src_ref=part.at[j, block(which, 0)], dst_ref=fin.at[which, :, cols(j)],
            send_sem=fin_s.at[2 * j + which], recv_sem=fin_r.at[2 * j + which],
            device_id=heirs[which], device_id_type=MESH,
        )
        copy.start()
        handed.append(copy)

    handed = []

    def rs_actions(j):
        e = 1 if j % 2 == 0 else -1
        fore, back = (ZP, ZM) if e == 1 else (ZM, ZP)

        def begin():
            weight_ready(1 + NC + j)
            out_project(j, 0)
            rs_send(j, OTHER, 4, YY, YE[4])
            rs_send(j, OTHER, -3 * e, back, QB[2])

        def cross(d):
            return lambda: rs_send(j, OTHER, d * e, YY, YE[d])

        def relay(kind, d, slots, way, slot):
            def act():
                rs_add(j, kind, d, slots)
                rs_send(j, kind, d, way, slot)

            return act

        def finish(kind, slots):
            def act():
                rs_add(j, kind, 0, slots)
                hand_on(j, kind)

            return act

        return [
            (0, begin),
            (RS_Y[0], cross(3)),
            (RS_Y[0] + 0.06, lambda: out_project(j, 1)),
            (RS_Y[1], cross(2)),
            (RS_Y[2], cross(1)),
            (T_B[0], lambda: rs_send(j, SAME, -3 * e, back, RB[2])),
            (T_F[0], relay(SAME, 4, [YE[4]], fore, RF[3])),
            (T_Q[0], relay(OTHER, -2 * e, [QB[2]], back, QB[1])),
            (T_B[1], relay(SAME, -2 * e, [RB[2]], back, RB[1])),
            (T_F[1], relay(SAME, 3 * e, [YE[3], RF[3]], fore, RF[2])),
            (T_Q[1], relay(OTHER, -e, [QB[1]], back, QB[0])),
            (T_B[2], relay(SAME, -e, [RB[1]], back, RB[0])),
            (T_F[2], relay(SAME, 2 * e, [YE[2], RF[2]], fore, RF[1])),
            (RS_Q, finish(OTHER, [QB[0]])),
            (T_F[3], relay(SAME, e, [YE[1], RF[1]], fore, RF[0])),
            (5, finish(SAME, [RF[0], RB[0]])),
        ]

    actions = [(RS_Y[0] + 0.05, lambda: attend(1, mask_of(1)))]
    for j in range(NC):
        actions += [(j * RS_LAP + when, act) for when, act in rs_actions(j)]
    for _, act in sorted(actions, key=lambda item: item[0]):
        act()

    for j in range(NC):
        for which in range(2):
            ref = fin.at[which, :, cols(j)]
            pltpu.make_async_remote_copy(
                src_ref=ref, dst_ref=ref,
                send_sem=fin_s.at[0], recv_sem=fin_r.at[2 * j + which],
                device_id=heirs[0], device_id_type=MESH,
            ).wait_recv()

    for copy in sends:
        copy.wait_send()
    for copy in far:
        copy.wait_send()
    for mine, copy in kv_copies:

        @pl.when(jnp.logical_not(mine))
        def _(copy=copy):
            copy.wait_send()

    carry.wait()
    for copy in handed:
        copy.wait_send()


def finish_kernel(carried, sums, next_resid, next_output):
    next_resid[...] = carried[...]
    next_output[...] = (sums[0].astype(F32) + sums[1].astype(F32)).astype(BF16)


def body(resid, pending, doc_ids, norm_gain, q_weight, kv_weight, o_weight):
    vmem = pl.BlockSpec(memory_space=pltpu.VMEM)
    hbm = pl.BlockSpec(memory_space=pltpu.HBM)
    dma = pltpu.SemaphoreType.DMA
    carried, sums = pl.pallas_call(
        kernel,
        out_shape=(
            jax.ShapeDtypeStruct((ROWS, D), BF16),
            jax.ShapeDtypeStruct((2, ROWS, D), BF16),
        ),
        in_specs=[vmem] * 4 + [hbm] * 3,
        out_specs=(hbm, hbm),
        scratch_shapes=[
            pltpu.VMEM((NC, TOK, KC), BF16),
            pltpu.VMEM((2, D, 256), BF16),
            pltpu.VMEM((64, D), BF16),
            pltpu.VMEM((512, D), BF16),
            pltpu.VMEM((TOK, 512), F32),
            pltpu.VMEM((64, TOK), F32),
            pltpu.VMEM((64, TOK), BF16),
            pltpu.VMEM((2, 256, TOK), BF16),
            pltpu.VMEM((2, TOK // 2, 512), BF16),
            pltpu.VMEM((NC, TOK, KC), BF16),
            pltpu.VMEM((NC, SLOTS, ROWS, KC), BF16),
            pltpu.VMEM((ROWS, D), BF16),
            dma((NC * 16,)),
            dma((NC * 16,)),
            dma((NC * 20,)),
            dma((NC * SLOTS,)),
            dma((10,)),
            dma((8,)),
            dma((1 + 2 * NC,)),
            dma((1 + 2 * NC,)),
            dma((1 + 2 * NC,)),
            dma,
            dma,
            dma((2 * NC,)),
            dma((2 * NC,)),
        ],
        compiler_params=pltpu.CompilerParams(
            collective_id=0, has_side_effects=True, vmem_limit_bytes=VMEM << 20
        ),
        name="module",
    )(
        resid[0], pending[0], doc_ids, norm_gain,
        q_weight[0], kv_weight[0].T, o_weight[0],
    )
    out = jax.ShapeDtypeStruct((ROWS, D), BF16)
    next_resid, next_output = pl.pallas_call(
        finish_kernel,
        out_shape=(out, out),
        in_specs=[vmem, vmem],
        out_specs=(vmem, vmem),
        compiler_params=pltpu.CompilerParams(vmem_limit_bytes=VMEM << 20),
        name="finish",
    )(carried, sums)
    return next_resid[None], next_output[None]


def solution(mesh):
    in_specs = (
        P("section", "tp", None),
        P("section", "tp", None),
        P("section", None),
        P("section", None),
        P("section", None, "tp"),
        P("section", None, "tp"),
        P("section", "tp", None),
    )
    out_specs = (P("section", "tp", None), P("section", "tp", None))
    return jax.shard_map(body, mesh=mesh, in_specs=in_specs, out_specs=out_specs, check_vma=False)
```

```python
import functools
import jax
import jax.numpy as jnp
from jax import lax
from jax.experimental import pallas as pl
from jax.experimental.pallas import tpu as pltpu
from jax.sharding import PartitionSpec as P

D = 8192
HD = 128
Z = 8
ROWS = 16
TOK = 256
NC = 4
KC = D // NC
VMEM = 56
AG_LAP = 0.25
AG_LAG = 1.1
KV_ORDER = (0, 1, 2, 3)
T_F = (1, 2, 3, 4)
T_Q = (1, 2)
T_B = (0, 1.5, 2.5)
AG_MM = 0.5
RS_LAP = 0
RS_Q = 2.5
FIN_LAG = 1.5
RS_Y = (0.1, 0.2, 0.3)
MESH = pl.DeviceIdType.MESH
F32 = jnp.float32
BF16 = jnp.bfloat16
SAME, OTHER = 0, 1
ZP, ZM, YY = 0, 1, 2

YE = {4: 0, 3: 1, 2: 2, 1: 3}
RF = {3: 4, 2: 5, 1: 6, 0: 7}
RB = {2: 8, 1: 9, 0: 10}
QB = {2: 11, 1: 12, 0: 13}
SLOTS = 14


def kernel(
    resid, pending, doc_ids, gain, wq_hbm, wkv_hbm, wo_hbm,
    next_resid, fin,
    xg, wq, wkv, wo, accq, acckv, kvs, kvr, ctx, part, rsb, carr,
    ag_s, ag_r, rs_s, rs_r, kv_s, kv_r, lw, ws, wr, sh_s, sh_r, fin_s, fin_r,
):
    sec = lax.axis_index("section")
    t = lax.axis_index("tp")
    z, yh, c = t // 4, (t // 2) % 2, t % 2

    def at(zz, yy, cc):
        return (sec, (zz * 2 + yy) * 2 + cc)

    neighbour = (
        at((z + 1) % Z, yh, c),
        at((z + Z - 1) % Z, yh, c),
        at(z, 1 - yh, c),
    )
    sibling = at(z, yh, 1 - c)
    across = (z * 2 + 1 - yh) * 2 + c
    after, before = (sec + 1) % 8, (sec + 7) % 8
    heirs = ((after, t), (after, across))

    def block(kind, d):
        b = ((z + d + Z) % Z) * 2 + (yh if kind == SAME else 1 - yh)
        return pl.ds(pl.multiple_of(b * ROWS, ROWS), ROWS)

    barrier = pltpu.get_barrier_semaphore()
    for o in range(2, 32, 2):
        pl.semaphore_signal(barrier, inc=1, device_id=(sec, (t + o) % 32), device_id_type=MESH)
    for dev in (sibling, *heirs, (before, t), (before, across)):
        pl.semaphore_signal(barrier, inc=1, device_id=dev, device_id_type=MESH)

    def cols(j):
        return pl.ds(j * KC, KC)

    pieces = [(wkv_hbm, wkv.at[pl.ds(pl.multiple_of(c * 32, 32), 32)])]
    for j in range(NC):
        pieces.append((wq_hbm.at[cols(j)], wq.at[c, cols(j)]))
    for j in range(NC):
        pieces.append(
            (wo_hbm.at[:, cols(j)], wo.at[pl.ds(pl.multiple_of(c * 256, 256), 256), cols(j)])
        )
    local = [pltpu.make_async_copy(s, d, lw.at[i]) for i, (s, d) in enumerate(pieces)]
    far = [
        pltpu.make_async_remote_copy(
            src_ref=s, dst_ref=d, send_sem=ws.at[i], recv_sem=wr.at[i],
            device_id=sibling, device_id_type=MESH,
        )
        for i, (s, d) in enumerate(pieces)
    ]
    for copy in local:
        copy.start()

    stream = resid[...].astype(F32)
    scale = lax.rsqrt(jnp.mean(stream * stream, axis=-1, keepdims=True) + 1e-05)
    pl.semaphore_wait(barrier, 20)

    sends = []

    count = [0] * NC

    def ag_send(j, kind, d, way):
        dd = d - 1 if way == ZP else d + 1 if way == ZM else d
        kk = kind if way != YY else 1 - kind
        ref = xg.at[j, block(kind, d)]
        copy = pltpu.make_async_remote_copy(
            src_ref=ref, dst_ref=ref,
            send_sem=ag_s.at[j * 16 + count[j]], recv_sem=ag_r.at[j * 16 + kk * 8 + dd % 8],
            device_id=neighbour[way], device_id_type=MESH,
        )
        count[j] += 1
        copy.start()
        sends.append(copy)

    def ag_wait(j, kind, d):
        ref = xg.at[j, block(kind, d)]
        pltpu.make_async_remote_copy(
            src_ref=ref, dst_ref=ref,
            send_sem=ag_s.at[j * 16], recv_sem=ag_r.at[j * 16 + kind * 8 + d % 8],
            device_id=neighbour[YY], device_id_type=MESH,
        ).wait_recv()

    def ag_actions(j):
        e = 1 if j % 2 == 0 else -1
        fore, back = (ZP, ZM) if e == 1 else (ZM, ZP)

        def begin():
            piece = resid[:, j * KC : (j + 1) * KC].astype(F32)
            xg[j, block(SAME, 0)] = (
                piece * scale * gain[:, j * KC : (j + 1) * KC].astype(F32)
            ).astype(BF16)
            for way in (back, fore, YY):
                ag_send(j, SAME, 0, way)

        def relay(kind, d, *ways):
            def act():
                ag_wait(j, kind, d)
                for way in ways:
                    ag_send(j, kind, d, way)

            return act

        def finish():
            for kind, d in ((SAME, -3), (OTHER, 1), (OTHER, 2), (OTHER, 3), (OTHER, -3), (OTHER, 4)):
                ag_wait(j, kind, d * e if d != 4 else 4)

        return [
            (0, begin),
            (1, relay(SAME, e, back, YY)),
            (1, relay(SAME, -e, fore)),
            (1 + AG_LAG, relay(OTHER, 0, fore)),
            (2, relay(SAME, 2 * e, back, YY)),
            (2, relay(SAME, -2 * e, fore)),
            (2 + AG_LAG, relay(OTHER, -e, fore)),
            (3, relay(SAME, 3 * e, back, YY)),
            (3 + AG_LAG, relay(OTHER, -2 * e, fore)),
            (4, relay(SAME, 4, YY)),
            (5, finish),
        ]

    def weight_ready(i):
        local[i].wait()
        far[i].wait_recv()

    def project_kv(j):
        if j == 0:
            weight_ready(0)
        term = lax.dot_general(
            wkv[:, j * KC : (j + 1) * KC], xg[j], (((1,), (1,)), ((), ())),
            preferred_element_type=F32,
        )
        acckv[...] = term if j == 0 else acckv[...] + term

    def project_q(j):
        weight_ready(1 + j)
        for cc in range(2):
            term = jnp.dot(
                xg[j], wq[cc, j * KC : (j + 1) * KC, :], preferred_element_type=F32
            )
            span = slice(cc * 256, (cc + 1) * 256)
            accq[:, span] = term if j == 0 else accq[:, span] + term

    carry = pltpu.make_async_remote_copy(
        src_ref=carr, dst_ref=next_resid,
        send_sem=sh_s, recv_sem=sh_r,
        device_id=heirs[0], device_id_type=MESH,
    )

    def send_carry():
        carr[...] = (resid[...].astype(F32) + pending[...].astype(F32)).astype(BF16)
        carry.start()

    def send_weights():
        for copy in far:
            copy.start()

    def project(j):
        return lambda: project_kv(j)

    actions = [(0, send_weights)]
    for j in range(NC):
        actions += [(j * AG_LAP + when, act) for when, act in ag_actions(j)]
        if j < NC - 1:
            actions.append((j * AG_LAP + 5 + AG_MM, project(j)))
    for _, act in sorted(actions, key=lambda item: item[0]):
        act()

    project_kv(NC - 1)
    kvs[...] = acckv[...].astype(BF16)
    kv_rows = pl.ds(pl.multiple_of((z // 4) * 128 + yh * 64, 64), 64)
    kv_copies = []
    for n in range(4):
        zz, yy = 2 * (z % 4) + (n // 2 + 1 - z // 4) % 2, (n + 1 + yh) % 2
        mine = (zz == z) & (yy == yh)
        copy = pltpu.make_async_remote_copy(
            src_ref=kvs, dst_ref=kvr.at[c, kv_rows],
            send_sem=kv_s.at[n], recv_sem=kv_r.at[z // 4 * 2 + yh],
            device_id=at(zz, yy, c), device_id_type=MESH,
        )
        kv_copies.append((mine, copy))

        @pl.when(mine)
        def _():
            pltpu.make_async_copy(kvs, kvr.at[c, kv_rows], kv_r.at[z // 4 * 2 + yh]).start()

        @pl.when(jnp.logical_not(mine))
        def _(copy=copy):
            copy.start()

    for j in range(NC - 1):
        project_q(j)

    docs = doc_ids[...].astype(F32)
    key = lax.broadcasted_iota(jnp.int32, (1, 2 * TOK), 1)
    key_at = (((key % TOK) // 16) * 32 + (key // TOK) * 16 + key % 16).astype(F32)
    begins = [
        jnp.sum(jnp.where(docs < k, 1.0, 0.0), axis=-1, keepdims=True) for k in range(1, 4)
    ]

    def planes(g):
        return [
            pl.ds(pl.multiple_of((z + 2 + 4 * g + k) % Z * 32, 32), 32) for k in range(4)
        ]

    def mask_of(g):
        row = lax.broadcasted_iota(jnp.int32, (TOK // 2, 1), 0)
        plane = (z + 2 + 4 * g + row // 32) % Z
        mine_at = (plane * 64 + row % 32 // 16 * 32 + c * 16 + row % 16).astype(F32)
        first = jnp.zeros((TOK // 2, 1), F32)
        for begin in begins:
            first = jnp.maximum(first, jnp.where(mine_at >= begin, begin, 0.0))
        return (key_at <= mine_at) & (key_at >= first)

    mask = mask_of(0)

    def kv_relay(i, kind, half, targets):
        rows = pl.ds(kind * 128 + half * 64, 64)
        ref = kvr.at[c, rows]
        pltpu.make_async_remote_copy(
            src_ref=ref, dst_ref=ref, send_sem=kv_s.at[0], recv_sem=kv_r.at[i],
            device_id=sibling, device_id_type=MESH,
        ).wait_recv()
        for dev, slot in targets:
            copy = pltpu.make_async_remote_copy(
                src_ref=ref, dst_ref=ref,
                send_sem=kv_s.at[4 + i], recv_sem=kv_r.at[slot],
                device_id=dev, device_id_type=MESH,
            )
            copy.start()
            sends.append(copy)

    send_carry()
    project_q(NC - 1)
    for i in KV_ORDER:
        kv_relay(i, i // 2, i % 2, [(sibling, 4 + i)])
    for i in range(4):
        rows = pl.ds(i * 64, 64)
        ref = kvr.at[1 - c, rows]
        pltpu.make_async_remote_copy(
            src_ref=ref, dst_ref=ref, send_sem=kv_s.at[0], recv_sem=kv_r.at[4 + i],
            device_id=sibling, device_id_type=MESH,
        ).wait_recv()

    keys = jnp.concatenate([kvr[0, :128, :], kvr[1, :128, :]], axis=1)
    values = jnp.concatenate([kvr[0, 128:, :], kvr[1, 128:, :]], axis=1)
    def attend(g, mask):
        for h in range(4):
            span = slice(h * HD, (h + 1) * HD)
            query = jnp.concatenate([accq[rows, span] for rows in planes(g)], axis=0).astype(BF16)
            scores = jnp.dot(query, keys, preferred_element_type=F32) * HD**-0.5
            scores = jnp.where(mask, scores, -1e30)
            top = jnp.max(scores, axis=-1, keepdims=True)
            weight = jnp.exp(scores - top)
            probs = (weight * (1.0 / jnp.sum(weight, axis=-1, keepdims=True))).astype(BF16)
            ctx[g, :, span] = lax.dot_general(
                probs, values, (((1,), (1,)), ((), ())), preferred_element_type=F32
            ).astype(BF16)

    def out_project(j, g):
        for n in range(0, KC, 512):
            term = jnp.dot(
                ctx[g], wo[:, j * KC + n : j * KC + n + 512], preferred_element_type=F32
            ).astype(BF16)
            for k, rows in enumerate(planes(g)):
                part[j, rows, n : n + 512] = term[k * 32 : (k + 1) * 32]

    attend(0, mask)

    sent = [0] * NC

    def rs_send(j, kind, d, way, slot):
        copy = pltpu.make_async_remote_copy(
            src_ref=part.at[j, block(kind, d)], dst_ref=rsb.at[j, slot],
            send_sem=rs_s.at[j * 20 + sent[j]], recv_sem=rs_r.at[j * SLOTS + slot],
            device_id=neighbour[way], device_id_type=MESH,
        )
        sent[j] += 1
        copy.start()
        sends.append(copy)

    def rs_add(j, kind, d, slots):
        for slot in slots:
            ref = rsb.at[j, slot]
            pltpu.make_async_remote_copy(
                src_ref=ref, dst_ref=ref,
                send_sem=rs_s.at[j * 20], recv_sem=rs_r.at[j * SLOTS + slot],
                device_id=neighbour[YY], device_id_type=MESH,
            ).wait_recv()
        total = part[j, block(kind, d)].astype(F32)
        for slot in slots:
            total = total + rsb[j, slot].astype(F32)
        part[j, block(kind, d)] = total.astype(BF16)

    def hand_on(j, which):
        copy = pltpu.make_async_remote_copy(
            src_ref=part.at[j, block(which, 0)], dst_ref=fin.at[which, :, cols(j)],
            send_sem=fin_s.at[2 * j + which], recv_sem=fin_r.at[2 * j + which],
            device_id=heirs[which], device_id_type=MESH,
        )
        copy.start()
        handed.append(copy)

    handed = []

    def rs_actions(j):
        e = 1 if j % 2 == 0 else -1
        fore, back = (ZP, ZM) if e == 1 else (ZM, ZP)

        def begin():
            weight_ready(1 + NC + j)
            out_project(j, 0)
            rs_send(j, OTHER, 4, YY, YE[4])
            rs_send(j, OTHER, -3 * e, back, QB[2])

        def cross(d):
            return lambda: rs_send(j, OTHER, d * e, YY, YE[d])

        def relay(kind, d, slots, way, slot):
            def act():
                rs_add(j, kind, d, slots)
                rs_send(j, kind, d, way, slot)

            return act

        def finish(kind, slots):
            def act():
                rs_add(j, kind, 0, slots)
                hand_on(j, kind)

            return act

        return [
            (0, begin),
            (RS_Y[0], cross(3)),
            (RS_Y[0] + 0.06, lambda: out_project(j, 1)),
            (RS_Y[1], cross(2)),
            (RS_Y[2], cross(1)),
            (T_B[0], lambda: rs_send(j, SAME, -3 * e, back, RB[2])),
            (T_F[0], relay(SAME, 4, [YE[4]], fore, RF[3])),
            (T_Q[0], relay(OTHER, -2 * e, [QB[2]], back, QB[1])),
            (T_B[1], relay(SAME, -2 * e, [RB[2]], back, RB[1])),
            (T_F[1], relay(SAME, 3 * e, [YE[3], RF[3]], fore, RF[2])),
            (T_Q[1], relay(OTHER, -e, [QB[1]], back, QB[0])),
            (T_B[2], relay(SAME, -e, [RB[1]], back, RB[0])),
            (T_F[2], relay(SAME, 2 * e, [YE[2], RF[2]], fore, RF[1])),
            (RS_Q, finish(OTHER, [QB[0]])),
            (T_F[3] + j / 100, relay(SAME, e, [YE[1], RF[1]], fore, RF[0])),
            (T_F[3] + (j + FIN_LAG) / 100, finish(SAME, [RF[0], RB[0]])),
        ]

    actions = [(RS_Y[0] + 0.05, lambda: attend(1, mask_of(1)))]
    for j in range(NC):
        actions += [(j * RS_LAP + when, act) for when, act in rs_actions(j)]
    for _, act in sorted(actions, key=lambda item: item[0]):
        act()

    for j in range(NC):
        for which in range(2):
            ref = fin.at[which, :, cols(j)]
            pltpu.make_async_remote_copy(
                src_ref=ref, dst_ref=ref,
                send_sem=fin_s.at[0], recv_sem=fin_r.at[2 * j + which],
                device_id=heirs[0], device_id_type=MESH,
            ).wait_recv()

    for copy in sends:
        copy.wait_send()
    for copy in far:
        copy.wait_send()
    for mine, copy in kv_copies:

        @pl.when(jnp.logical_not(mine))
        def _(copy=copy):
            copy.wait_send()

    carry.wait()
    for copy in handed:
        copy.wait_send()


def finish_kernel(carried, sums, next_resid, next_output):
    next_resid[...] = carried[...]
    next_output[...] = (sums[0].astype(F32) + sums[1].astype(F32)).astype(BF16)


def body(resid, pending, doc_ids, norm_gain, q_weight, kv_weight, o_weight):
    vmem = pl.BlockSpec(memory_space=pltpu.VMEM)
    hbm = pl.BlockSpec(memory_space=pltpu.HBM)
    dma = pltpu.SemaphoreType.DMA
    carried, sums = pl.pallas_call(
        kernel,
        out_shape=(
            jax.ShapeDtypeStruct((ROWS, D), BF16),
            jax.ShapeDtypeStruct((2, ROWS, D), BF16),
        ),
        in_specs=[vmem] * 4 + [hbm] * 3,
        out_specs=(hbm, hbm),
        scratch_shapes=[
            pltpu.VMEM((NC, TOK, KC), BF16),
            pltpu.VMEM((2, D, 256), BF16),
            pltpu.VMEM((64, D), BF16),
            pltpu.VMEM((512, D), BF16),
            pltpu.VMEM((TOK, 512), F32),
            pltpu.VMEM((64, TOK), F32),
            pltpu.VMEM((64, TOK), BF16),
            pltpu.VMEM((2, 256, TOK), BF16),
            pltpu.VMEM((2, TOK // 2, 512), BF16),
            pltpu.VMEM((NC, TOK, KC), BF16),
            pltpu.VMEM((NC, SLOTS, ROWS, KC), BF16),
            pltpu.VMEM((ROWS, D), BF16),
            dma((NC * 16,)),
            dma((NC * 16,)),
            dma((NC * 20,)),
            dma((NC * SLOTS,)),
            dma((10,)),
            dma((8,)),
            dma((1 + 2 * NC,)),
            dma((1 + 2 * NC,)),
            dma((1 + 2 * NC,)),
            dma,
            dma,
            dma((2 * NC,)),
            dma((2 * NC,)),
        ],
        compiler_params=pltpu.CompilerParams(
            collective_id=0, has_side_effects=True, vmem_limit_bytes=VMEM << 20
        ),
        name="module",
    )(
        resid[0], pending[0], doc_ids, norm_gain,
        q_weight[0], kv_weight[0].T, o_weight[0],
    )
    out = jax.ShapeDtypeStruct((ROWS, D), BF16)
    next_resid, next_output = pl.pallas_call(
        finish_kernel,
        out_shape=(out, out),
        in_specs=[vmem, vmem],
        out_specs=(vmem, vmem),
        compiler_params=pltpu.CompilerParams(vmem_limit_bytes=VMEM << 20),
        name="finish",
    )(carried, sums)
    return next_resid[None], next_output[None]


def solution(mesh):
    in_specs = (
        P("section", "tp", None),
        P("section", "tp", None),
        P("section", None),
        P("section", None),
        P("section", None, "tp"),
        P("section", None, "tp"),
        P("section", "tp", None),
    )
    out_specs = (P("section", "tp", None), P("section", "tp", None))
    return jax.shard_map(body, mesh=mesh, in_specs=in_specs, out_specs=out_specs, check_vma=False)
```
